256 devices in a mesh: section: 16 (over z, core), dp: 16 (over y, x).
Axes of the slice: x: 4, y: 4, z: 8, core: 2. Of those that a mesh axis runs over, the one named last changes fastest.
Arguments:
- inputs: bfloat16 [2, 256, 1024], P(None, 'dp'), may hold values from -6 to 6, as said below
- norm_gain: float32 [16, 1024], P('section'), may hold values from 0.1 to 1.9
- w_query: bfloat16 [16, 1024, 8192], P('section', None, 'dp'), may hold values from -0.1875 to 0.1875
- w_key: bfloat16 [16, 1024, 8192], P('section', None, 'dp'), may hold values from -12.5 to 12.5
- w_value: bfloat16 [16, 1024, 8192], P('section', None, 'dp'), may hold values from -0.1875 to 0.1875
- w_output: bfloat16 [16, 8192, 1024], P('section', 'dp'), may hold values from -0.0625 to 0.0625
- segment_ids: int32 [2, 256], replicated, may hold values from 0 to 7, never falling along the last dimension, each value on 1 to 64 neighbouring positions
- prefix_lengths: int32 [2, 8], replicated, may hold values from 1 to 64
- batch_lengths: int32 [2], replicated, may hold values from 128 to 256, as said below
Outputs:
- stashed: bfloat16 [16, 2, 256, 1024], P('section', None, 'dp')
The draws below stay inside these ranges and needn't reach their ends.
Inputs may be any that keep to these rules, and one draw needn't show every extreme that they name: inputs are of order one. `segment_ids`: ids never fall along a micro-batch; each of the 8 ids holds 1 to 64 slots. `batch_lengths`: slots from the length on are padding; some micro-batch is full.
All inputs are finite; a program needn't handle non-finite values.
Results may differ from the reference program's by a relative error of at most 0.04.
Values may be sent and summed in bfloat16 or wider, within the bound.
No kernel may reach another device: no remote copies, remote signals or barrier semaphores. Data moves between devices by JAX's collectives and lax.ppermute only.
A program may use at most 64 MiB of HBM per device.

```python
import math
import jax
import jax.numpy as jnp
import numpy as np
from jax import lax

D = 1024
H = 64
DH = 128
L = 256
M = 2
NSEG = 8
LAYERS = 16
N_DP = 16


def shared_query(key):
    base = jax.random.normal(jax.random.fold_in(key, 11), (LAYERS, D, H * DH), jnp.float32)
    return jnp.clip(base, -6.0, 6.0) * D ** (-0.5)


def draw_w_query(key, part):
    base = shared_query(key)
    return base.astype(jnp.bfloat16)


def draw_w_key(key, part):
    key = jax.random.fold_in(key, 2)
    fresh = jnp.clip(jax.random.normal(key, (LAYERS, D, H * DH), jnp.float32), -6.0, 6.0) * D ** (-0.5)
    return fresh.astype(jnp.bfloat16)


def draw_inputs(key, part):
    key = jax.random.fold_in(key, 3)
    return jnp.clip(jax.random.normal(key, (M, L, D), jnp.float32), -6.0, 6.0).astype(jnp.bfloat16)


def draw_batch_lengths(key, part):
    key = jax.random.fold_in(key, 4)
    base = jax.random.randint(key, (M,), L // 2, L + 1, dtype=jnp.int32)
    chosen = jax.random.randint(jax.random.fold_in(key, 5), (), 0, M, dtype=jnp.int32)
    return jnp.where(jnp.arange(M, dtype=jnp.int32) == chosen, jnp.int32(L), base)


def with_ends(entries, stream_key, low, top_value):
    extent = entries.shape
    spot = [jax.random.randint(jax.random.fold_in(stream_key, axis), (), 0, extent[axis]) for axis in range(len(extent))]
    entries = entries.at[tuple(spot)].set(low)
    longest = extent.index(max(extent))
    spot[longest] = (spot[longest] + 1) % extent[longest]
    return entries.at[tuple(spot)].set(top_value)


def block_levels(rng, extent, cuts, least, high):
    def one(dim, shards_of):
        draws = jax.random.uniform(jax.random.fold_in(jax.random.fold_in(rng, 6), dim), (shards_of,), jnp.float32, least / len(cuts), high / len(cuts))
        return jnp.repeat(jnp.exp(draws), extent[dim] // shards_of).reshape((-1,) + (1,) * (len(extent) - dim - 1))

    loudness = one(*cuts[0])
    for cut in cuts[1:]:
        loudness = loudness * one(*cut)
    return loudness


def profile(count, total, reach, skew):
    portions = [(1 << 20) // math.isqrt(standing ** skew) + 1 for standing in range(2, count + 1)]
    rest, holding = total - reach - (count - 1), [1] * (count - 1)
    while rest > 0:
        candidates = [i for i in range(count - 1) if holding[i] < reach]
        pool, remaining = sum([portions[i] for i in candidates]), rest
        for i in candidates:
            addition = min(reach - holding[i], max(1, remaining * portions[i] // pool), rest)
            holding[i] = holding[i] + addition
            rest = rest - addition
    return np.array([reach] + holding)


def uneven(own_key, number_of, total, limit, slope):
    if number_of == 2:
        one = jax.random.randint(own_key, (), max(1, total - limit), min(limit, total - 1) + 1)
        return jnp.stack([one, total - one])
    sizes = jnp.asarray(profile(number_of, total, limit, slope), jnp.int32)
    couples = (number_of - 1) // 2
    giver, sink = sizes[1:1 + 2 * couples:2], sizes[2:2 + 2 * couples:2]
    slack = jnp.minimum(giver - 1, limit - sink)
    moved = jax.random.randint(jax.random.fold_in(own_key, 1), (couples,), 0, 1 << 20) % (slack + 1)
    sizes = sizes.at[1:1 + 2 * couples:2].set(giver - moved).at[2:2 + 2 * couples:2].set(sink + moved)
    return sizes[jax.random.permutation(jax.random.fold_in(own_key, 2), number_of)]


def bell_draw(rng, extent, scale, reach, shards=(), held_as=jnp.bfloat16):
    result = scale * jax.random.normal(rng, extent, jnp.float32)
    if shards:
        result = result * block_levels(rng, extent, shards, -0.22, 0.18)
    return jnp.clip(result, -reach, reach).astype(held_as)


def setup_inputs(seed: int = 0) -> dict:
    streams_of = jax.random.split(jax.random.key(seed), 10)
    inputs = draw_inputs(jax.random.fold_in(streams_of[9], 71), 0)
    norm_gain = jnp.clip(1.0 + 0.18 * jax.random.normal(streams_of[1], (LAYERS, D), jnp.float32), 0.1, 1.9)
    w_query = draw_w_query(jax.random.fold_in(streams_of[9], 71), 0)
    w_key = draw_w_key(jax.random.fold_in(streams_of[9], 71), 0)
    w_value = bell_draw(streams_of[4], (LAYERS, D, H * DH), D ** -0.5, 0.1875, ((0, 16), (2, 16)))
    w_output = bell_draw(streams_of[5], (LAYERS, H * DH, D), (H * DH) ** -0.5, 0.0625, ((0, 16), (1, 16)))
    segment_ids = jax.vmap(lambda own: jnp.searchsorted(jnp.cumsum(uneven(own, NSEG, L, L // 4, 1)), jnp.arange(L), side="right"))(jax.random.split(streams_of[6], M)).reshape((M, L)).astype(jnp.int32)
    prefix_lengths = with_ends(jax.random.randint(streams_of[7], (M, NSEG), 1, L // 4 + 1), jax.random.fold_in(streams_of[7], 1), 1, (L // 4 + 1) - 1).astype(jnp.int32)
    batch_lengths = draw_batch_lengths(jax.random.fold_in(streams_of[9], 71), 0)
    return dict(inputs=inputs, norm_gain=norm_gain, w_query=w_query, w_key=w_key, w_value=w_value, w_output=w_output, segment_ids=segment_ids, prefix_lengths=prefix_lengths, batch_lengths=batch_lengths)


def rms_scale(hidden, norm_gain):
    wide = hidden.astype(jnp.float32)
    mean_square = lax.optimization_barrier(jnp.mean(wide * wide, axis=-1, keepdims=True))
    return (wide * lax.rsqrt(mean_square + 1e-06) * norm_gain.astype(jnp.float32)).astype(jnp.bfloat16)

def visible_keys(segments, prefixes, length):
    seq_len = segments.shape[0]
    count_seg = prefixes.shape[0]
    position = jnp.arange(seq_len, dtype=jnp.int32)
    member = segments[:, None] == jnp.arange(count_seg, dtype=jnp.int32)[None, :]
    seg_start = lax.optimization_barrier(jnp.min(jnp.where(member, position[:, None], jnp.int32(seq_len)), axis=0))
    prefix_end = lax.optimization_barrier(jnp.sum(jnp.where(member, (seg_start + prefixes)[None, :], jnp.int32(0)), axis=1))
    key_ok = (position[None, :] <= position[:, None]) | (position[None, :] < prefix_end[None, :])
    same_seg = segments[:, None] == segments[None, :]
    live_keys = (position[None, :] < length) | (position[None, :] == position[:, None])
    return same_seg & key_ok & live_keys

def one_layer(hidden, norm_gain, w_query, w_key, w_value, w_output, segments, prefixes, length):
    seq_len = hidden.shape[0]
    width = w_query.shape[1]
    heads = width // DH
    normed = rms_scale(hidden, norm_gain)
    queries = jnp.dot(normed, w_query, preferred_element_type=jnp.float32).astype(jnp.bfloat16).reshape(seq_len, heads, DH)
    keyed = jnp.dot(normed, w_key, preferred_element_type=jnp.float32).astype(jnp.bfloat16).reshape(seq_len, heads, DH)
    values = jnp.dot(normed, w_value, preferred_element_type=jnp.float32).astype(jnp.bfloat16).reshape(seq_len, heads, DH)
    scores = jnp.einsum('qhd,khd->hqk', queries.astype(jnp.float32), keyed.astype(jnp.float32)) * DH ** (-0.5)
    visible = visible_keys(segments, prefixes, length)
    scores = jnp.where(visible[None, :, :], scores, jnp.float32(-1e+30))
    row_max = lax.optimization_barrier(jnp.max(scores, axis=-1, keepdims=True))
    expo = jnp.exp(scores - row_max)
    weights = (expo / lax.optimization_barrier(jnp.sum(expo, axis=-1, keepdims=True))).astype(jnp.bfloat16)
    context = jnp.einsum('hqk,khd->qhd', weights.astype(jnp.float32), values.astype(jnp.float32))
    context = context.astype(jnp.bfloat16).reshape(seq_len, width)
    group_width = width // N_DP
    group_terms = jnp.einsum('lgw,gwd->gld', context.reshape(seq_len, N_DP, group_width).astype(jnp.float32), w_output.reshape(N_DP, group_width, w_output.shape[1]).astype(jnp.float32)).astype(jnp.bfloat16)
    group_terms = lax.optimization_barrier(group_terms)
    summed = lax.optimization_barrier(jnp.sum(group_terms.astype(jnp.float32), axis=0))
    live_rows = jnp.arange(seq_len, dtype=jnp.int32) < length
    return (hidden.astype(jnp.float32) + jnp.where(live_rows[:, None], summed, jnp.float32(0.0))).astype(jnp.bfloat16)

def reference(inputs, norm_gain, w_query, w_key, w_value, w_output, segment_ids, prefix_lengths, batch_lengths):

    def section_step(hidden_all, layer_weights):
        gain_one, query_one, key_one, value_one, output_one = layer_weights

        def per_micro(packed):
            return one_layer(packed[0], gain_one, query_one, key_one, value_one, output_one, packed[1], packed[2], packed[3])
        updated = lax.map(per_micro, (hidden_all, segment_ids, prefix_lengths, batch_lengths))
        return (updated, updated)
    _, stashed = lax.scan(section_step, inputs, (norm_gain, w_query, w_key, w_value, w_output))
    return stashed
```

```python
import jax
import jax.numpy as jnp
from jax import lax
from jax.sharding import PartitionSpec as P

DH = 128


def from_behind(value, axis, steps):
    count = lax.axis_size(axis)
    first, last = (max(0, -steps), min(count, count - steps))
    return lax.ppermute(value, axis, [(source, source + steps) for source in range(first, last)])


def rms_scale(hidden, norm_gain):
    wide = hidden.astype(jnp.float32)
    mean_square = jnp.mean(wide * wide, axis=-1, keepdims=True)
    return (wide * lax.rsqrt(mean_square + 1e-06) * norm_gain).astype(jnp.bfloat16)


def visible_keys(segments, prefixes, length):
    seq_len = segments.shape[0]
    count_seg = prefixes.shape[0]
    position = jnp.arange(seq_len, dtype=jnp.int32)
    member = segments[:, None] == jnp.arange(count_seg, dtype=jnp.int32)[None, :]
    seg_start = jnp.min(jnp.where(member, position[:, None], jnp.int32(seq_len)), axis=0)
    prefix_end = jnp.sum(jnp.where(member, (seg_start + prefixes)[None, :], jnp.int32(0)), axis=1)
    key_ok = (position[None, :] <= position[:, None]) | (position[None, :] < prefix_end[None, :])
    same_seg = segments[:, None] == segments[None, :]
    live_keys = (position[None, :] < length) | (position[None, :] == position[:, None])
    return same_seg & key_ok & live_keys


def head_terms(
    normed_all, query_here, key_here, value_here, output_here, segments, prefixes, length
):
    seq_len = normed_all.shape[0]
    width = query_here.shape[1]
    heads = width // DH
    queries = (
        jnp.dot(normed_all, query_here, preferred_element_type=jnp.float32)
        .astype(jnp.bfloat16)
        .reshape(seq_len, heads, DH)
    )
    keyed = (
        jnp.dot(normed_all, key_here, preferred_element_type=jnp.float32)
        .astype(jnp.bfloat16)
        .reshape(seq_len, heads, DH)
    )
    values = (
        jnp.dot(normed_all, value_here, preferred_element_type=jnp.float32)
        .astype(jnp.bfloat16)
        .reshape(seq_len, heads, DH)
    )
    scores = jnp.einsum(
        "qhd,khd->hqk", queries, keyed, preferred_element_type=jnp.float32
    ) * DH ** (-0.5)
    visible = visible_keys(segments, prefixes, length)
    scores = jnp.where(visible[None, :, :], scores, jnp.float32(-1e30))
    row_max = jnp.max(scores, axis=-1, keepdims=True)
    expo = jnp.exp(scores - row_max)
    weights = (expo / jnp.sum(expo, axis=-1, keepdims=True)).astype(jnp.bfloat16)
    context = jnp.einsum("hqk,khd->qhd", weights, values, preferred_element_type=jnp.float32)
    context = context.astype(jnp.bfloat16).reshape(seq_len, width)
    return jnp.dot(context, output_here, preferred_element_type=jnp.float32)


def shards(
    inputs, norm_gain, w_query, w_key, w_value, w_output, segment_ids, prefix_lengths, batch_lengths
):
    section_index = lax.axis_index("section")
    sections = lax.axis_size("section")
    groups = lax.axis_size("dp")
    group_index = lax.axis_index("dp")
    micro_count = inputs.shape[0]
    row_count = inputs.shape[1]
    model_width = inputs.shape[2]
    seq_len = row_count * groups
    gain_here = norm_gain[0]
    query_here = w_query[0]
    key_here = w_key[0]
    value_here = w_value[0]
    output_here = w_output[0]
    own_rows = group_index * row_count + jnp.arange(row_count, dtype=jnp.int32)
    tick_count = micro_count + sections - 1
    stash_start = jnp.zeros((micro_count, row_count, model_width), jnp.bfloat16)

    def run_heads(normed_all, micro, active):

        def busy(operand):
            return head_terms(
                operand,
                query_here,
                key_here,
                value_here,
                output_here,
                segment_ids[micro],
                prefix_lengths[micro],
                batch_lengths[micro],
            )

        def quiet(operand):
            return jnp.zeros((seq_len, model_width), jnp.float32)

        return lax.cond(active, busy, quiet, normed_all)

    def place_micro(tick_index):
        micro_raw = tick_index - section_index
        active = (micro_raw >= 0) & (micro_raw < micro_count)
        return (jnp.clip(micro_raw, 0, micro_count - 1), active)

    def finish_rows(layer_in, summed, micro):
        live_rows = own_rows < batch_lengths[micro]
        return (
            layer_in.astype(jnp.float32) + jnp.where(live_rows[:, None], summed, jnp.float32(0.0))
        ).astype(jnp.bfloat16)

    def keep_stash(stashed, layer_out, micro, active):
        written = lax.dynamic_update_index_in_dim(stashed, layer_out, micro, 0)
        return jnp.where(active, written, stashed)

    inputs_all = lax.all_gather(inputs, "dp", axis=1, tiled=True)

    def tick_whole(tick_index, loop_state):
        previous_all, stashed = loop_state
        incoming = from_behind(previous_all, "section", 1)
        micro, active = place_micro(tick_index)
        layer_in_all = jnp.where(section_index == 0, inputs_all[micro], incoming)
        normed_all = rms_scale(layer_in_all, gain_here)
        terms = run_heads(normed_all, micro, active)
        pieces = lax.all_to_all(
            terms.astype(jnp.bfloat16).reshape(groups, row_count, model_width), "dp", 0, 0
        )
        summed = jnp.sum(pieces.astype(jnp.float32), axis=0)
        layer_in = lax.dynamic_slice_in_dim(layer_in_all, group_index * row_count, row_count, 0)
        layer_out = finish_rows(layer_in, summed, micro)
        copies = jnp.broadcast_to(layer_out[None], (groups, row_count, model_width))
        layer_out_all = lax.all_to_all(copies, "dp", 0, 0).reshape(seq_len, model_width)
        return (layer_out_all, keep_stash(stashed, layer_out, micro, active))

    first_all = jnp.zeros((seq_len, model_width), jnp.bfloat16)
    _, stashed = lax.fori_loop(0, tick_count, tick_whole, (first_all, stash_start))
    return stashed[None]


def solution(mesh):
    return jax.shard_map(
        shards,
        mesh=mesh,
        in_specs=(
            P(None, "dp", None),
            P("section", None),
            P("section", None, "dp"),
            P("section", None, "dp"),
            P("section", None, "dp"),
            P("section", "dp", None),
            P(),
            P(),
            P(),
        ),
        out_specs=P("section", None, "dp", None),
        check_vma=False,
    )
```

```python
import functools

import jax
import jax.numpy as jnp
from jax import lax
from jax.experimental import pallas as pl
from jax.experimental.pallas import tpu as pltpu
from jax.sharding import PartitionSpec as P

DH = 128
SIDE = 4
WINDOW = 128
STARTS = (0, 32, 96, 128)


def layer_kernel(flag_ref, hidden_ref, gain_ref, bias_ref, live_ref, *refs):
    weights, out_ref = refs[:16], refs[16]

    @pl.when(flag_ref[0] > 0)
    def _():
        wide = hidden_ref[...].astype(jnp.float32)
        mean_square = jnp.mean(wide * wide, axis=-1, keepdims=True)
        normed = (wide * lax.rsqrt(mean_square + 1e-06) * gain_ref[...]).astype(jnp.bfloat16)
        bias = bias_ref[...]
        heads = weights[0].shape[1] // DH

        def project(ref):
            return jnp.dot(
                normed, ref[...], preferred_element_type=jnp.float32
            ).astype(jnp.bfloat16)

        def attend(queries, keyed, values):
            parts = []
            for head in range(heads):
                cols = slice(head * DH, (head + 1) * DH)
                scores = lax.dot_general(
                    queries[:, cols], keyed[:, cols], (((1,), (1,)), ((), ())),
                    preferred_element_type=jnp.float32,
                ) * DH ** (-0.5) + bias
                expo = jnp.exp(scores - jnp.max(scores, axis=-1, keepdims=True))
                weight = (expo / jnp.sum(expo, axis=-1, keepdims=True)).astype(jnp.bfloat16)
                parts.append(
                    jnp.dot(weight, values[:, cols], preferred_element_type=jnp.float32)
                    .astype(jnp.bfloat16)
                )
            return jnp.concatenate(parts, axis=1)

        total = None
        for j in range(SIDE):
            context = attend(*[project(ref) for ref in weights[4 * j : 4 * j + 3]])
            term = jnp.dot(
                context, weights[4 * j + 3][...], preferred_element_type=jnp.float32
            )
            total = term if total is None else total + term
        out_ref[...] = jnp.where(live_ref[...] > 0.0, total, 0.0).astype(out_ref.dtype)


def run_layer(flag, hidden, gain, bias, live, weights):
    rows, model = hidden.shape
    width = weights[0].shape[1]
    vmem = pl.BlockSpec(memory_space=pltpu.VMEM)
    return pl.pallas_call(
        layer_kernel,
        out_shape=jax.ShapeDtypeStruct((rows, model), jnp.bfloat16),
        in_specs=[pl.BlockSpec(memory_space=pltpu.SMEM)] + [vmem] * 20,
        out_specs=vmem,
        compiler_params=pltpu.CompilerParams(vmem_limit_bytes=32 * 1024 * 1024),
        cost_estimate=pl.CostEstimate(
            flops=2 * rows * model * width * 16, bytes_accessed=16 * model * width * 2,
            transcendentals=rows * rows * 16,
        ),
    )(flag, hidden, gain, bias, live, *weights)


def group_bounds(segments):
    seq_len = segments.shape[0]
    quarter = seq_len // SIDE
    position = jnp.arange(seq_len, dtype=jnp.int32)
    before = jnp.concatenate([segments[:1] - 1, segments[:-1]])
    begins = segments != before
    bounds = [jnp.int32(0)]
    for g in range(1, SIDE):
        middle = g * quarter
        low = jnp.max(jnp.where(begins & (position <= middle), position, 0))
        high = jnp.min(jnp.where(begins & (position >= middle), position, seq_len))
        bounds.append(jnp.where(middle - low <= high - middle, low, high))
    return jnp.stack(bounds)


def window_masks(segments, prefixes, length, start):
    seq_len = segments.shape[0]
    count_seg = prefixes.shape[0]
    position = jnp.arange(seq_len, dtype=jnp.int32)
    member = segments[:, None] == jnp.arange(count_seg, dtype=jnp.int32)[None, :]
    seg_start = jnp.min(jnp.where(member, position[:, None], jnp.int32(seq_len)), axis=0)
    prefix_end = jnp.sum(jnp.where(member, (seg_start + prefixes)[None, :], jnp.int32(0)), axis=1)
    seg_w = lax.dynamic_slice_in_dim(segments, start, WINDOW, 0)
    end_w = lax.dynamic_slice_in_dim(prefix_end, start, WINDOW, 0)
    pos_w = start + jnp.arange(WINDOW, dtype=jnp.int32)
    key_ok = (pos_w[None, :] <= pos_w[:, None]) | (pos_w[None, :] < end_w[None, :])
    live_keys = (pos_w[None, :] < length) | (pos_w[None, :] == pos_w[:, None])
    visible = (seg_w[:, None] == seg_w[None, :]) & key_ok & live_keys
    bias = jnp.where(visible, jnp.float32(0.0), jnp.float32(-1e30))
    live = (pos_w < length).astype(jnp.float32)[:, None]
    return bias, live


def everywhere(sections, groups, move):
    pairs = []
    for section in sections:
        for y in range(SIDE):
            for x in range(SIDE):
                there = move(section, y, x)
                if there is not None:
                    to, ty, tx = there
                    pairs.append(
                        (section * groups + y * SIDE + x,
                         to * groups + (ty % SIDE) * SIDE + tx % SIDE)
                    )
    return pairs


AXES = ("section", "dp")


def shards(
    inputs, norm_gain, w_query, w_key, w_value, w_output, segment_ids, prefix_lengths, batch_lengths
):
    section = lax.axis_index("section")
    sections = lax.axis_size("section")
    groups = lax.axis_size("dp")
    place = lax.axis_index("dp")
    micro_count, row_count, model = inputs.shape
    seq_len = row_count * groups
    quarter = seq_len // SIDE
    y, x = place // SIDE, place % SIDE
    group = (y + x) % SIDE
    start = jnp.asarray(STARTS, jnp.int32)[group]

    def ring(step):
        return everywhere(
            range(sections), groups,
            lambda s, a, b: (s, a + step, b) if s % 2 == 0 else (s, a, b + step),
        )

    own = [w_query[0], w_key[0], w_value[0], w_output[0]]
    ahead, behind = ring(1), ring(-1)
    from_low = [lax.ppermute(w, AXES, ahead) for w in own]
    from_high = [lax.ppermute(w, AXES, behind) for w in own]
    opposite = [lax.ppermute(w, AXES, ahead) for w in from_low[:2]]
    opposite += [lax.ppermute(w, AXES, behind) for w in from_high[2:]]
    weights = own + from_low + from_high + opposite

    inputs_all = lax.all_gather(inputs, "dp", axis=1, tiled=True)
    window_in = lax.dynamic_slice_in_dim(inputs_all, start, WINDOW, 1)

    masks = [
        window_masks(segment_ids[m], prefix_lengths[m], batch_lengths[m], start)
        for m in range(micro_count)
    ]
    biases = jnp.stack([m[0] for m in masks])
    lives = jnp.stack([m[1] for m in masks])

    own_from = quarter * group + row_count * x - start
    side_group = jnp.where(x < SIDE // 2, group + 1, group - 1)
    side_from = jnp.clip(quarter * side_group + row_count * x - start, 0, WINDOW - row_count)

    kept = [jnp.zeros((2, row_count, model), jnp.bfloat16)] * micro_count
    hidden = window_in[0]
    for tick in range(sections + micro_count - 1):
        busy = [s for s in (tick, tick - 1) if 0 <= s < sections]
        micro = jnp.clip(tick - section, 0, micro_count - 1)
        active = (section <= tick) & (section > tick - micro_count)
        partial = run_layer(
            active.astype(jnp.int32)[None], hidden, norm_gain, biases[micro], lives[micro], weights
        )
        arrived = [
            lax.ppermute(
                partial, AXES,
                everywhere(busy, groups, lambda s, a, b, k=k: (s, a + k, b - k)),
            )
            for k in range(1, SIDE)
        ]
        total = partial.astype(jnp.float32)
        for piece in arrived:
            total = total + piece.astype(jnp.float32)
        layer_out = (hidden.astype(jnp.float32) + total).astype(jnp.bfloat16)
        rows = jnp.stack([
            lax.dynamic_slice_in_dim(layer_out, own_from, row_count, 0),
            lax.dynamic_slice_in_dim(layer_out, side_from, row_count, 0),
        ])
        kept = [
            jnp.where(section == tick - m, rows, kept[m]) if 0 <= tick - m < sections else kept[m]
            for m in range(micro_count)
        ]
        onward = [s for s in busy if s + 1 < sections]
        if onward:
            hidden = lax.ppermute(
                layer_out, AXES, everywhere(onward, groups, lambda s, a, b: (s + 1, a, b))
            )
            if tick + 1 < micro_count:
                hidden = jnp.where(section == 0, window_in[tick + 1], hidden)

    stacked = jnp.stack(kept, axis=1)
    mine = lax.ppermute(
        stacked[0], AXES,
        everywhere(range(sections), groups, lambda s, a, b: (s, (a + b) % SIDE, b)),
    )

    def to_side(s, a, b):
        owner = (a + b) % SIDE + (1 if b < SIDE // 2 else -1)
        return (s, owner, b) if 0 <= owner < SIDE else None

    other = lax.ppermute(stacked[1], AXES, everywhere(range(sections), groups, to_side))
    slots = place * row_count + jnp.arange(row_count, dtype=jnp.int32)
    picked = []
    for m in range(micro_count):
        bounds = group_bounds(segment_ids[m])
        holder = jnp.sum((slots[:, None] >= bounds[None, 1:]).astype(jnp.int32), axis=1)
        picked.append(jnp.where((holder == y)[:, None], mine[m], other[m]))
    return jnp.stack(picked)[None]


def solution(mesh):
    return jax.shard_map(
        shards,
        mesh=mesh,
        in_specs=(
            P(None, "dp", None),
            P("section", None),
            P("section", None, "dp"),
            P("section", None, "dp"),
            P("section", None, "dp"),
            P("section", "dp", None),
            P(),
            P(),
            P(),
        ),
        out_specs=P("section", None, "dp", None),
        check_vma=False,
    )
```

```python
import jax
import jax.numpy as jnp
from jax import lax
from jax.experimental import pallas as pl
from jax.experimental.pallas import tpu as pltpu
from jax.sharding import PartitionSpec as P

DH = 128
SIDE = 4
WINDOW = 128
HALF = WINDOW // 2
STARTS = (0, 32, 96, 128)
AXES = ("section", "dp")


def layer_kernel(state_ref, mine_ref, other_ref, gain_ref, bias_ref, live_ref, *refs):
    own, from_x, from_y, top, bottom = refs[:5]
    keep_ref, send_ref, buf_in, buf_out, sem_in, sem_out = refs[5:]
    model, width = buf_in.shape[2:]

    def piece(j, n, row, rows):
        if j < 3:
            return (own, from_x, from_y)[j].at[pl.ds(n * model + row, rows)]
        source = top if n < 2 else bottom
        return source.at[pl.ds((n % 2) * model + row, rows)]

    def load_in(j, n):
        return pltpu.make_async_copy(piece(j, n, 0, model), buf_in.at[j, n], sem_in.at[j, n])

    def load_out(j, b):
        return pltpu.make_async_copy(
            piece(j, 3, b * width, width), buf_out.at[b, pl.ds(j * width, width)], sem_out.at[j, b]
        )

    @pl.when(state_ref[0] > 0)
    def _():
        for j in range(4):
            for n in range(3):
                load_in(j, n).start()
        for j in range(4):
            for b in range(4):
                load_out(j, b).start()

        wide = jnp.concatenate([mine_ref[...], other_ref[...]], axis=0).astype(jnp.float32)
        mean_square = jnp.mean(wide * wide, axis=-1, keepdims=True)
        normed = (wide * lax.rsqrt(mean_square + 1e-06) * gain_ref[...]).astype(jnp.bfloat16)
        bias = bias_ref[state_ref[1]]

        def project(j, n):
            load_in(j, n).wait()
            return jnp.dot(
                normed, buf_in[j, n], preferred_element_type=jnp.float32
            ).astype(jnp.bfloat16)

        context = []
        for j in range(4):
            queries, keyed, values = project(j, 0), project(j, 1), project(j, 2)
            for head in range(width // DH):
                cols = slice(head * DH, (head + 1) * DH)
                scores = lax.dot_general(
                    queries[:, cols], keyed[:, cols], (((1,), (1,)), ((), ())),
                    preferred_element_type=jnp.float32,
                ) * DH ** (-0.5) + bias
                expo = jnp.exp(scores - jnp.max(scores, axis=-1, keepdims=True))
                weight = (expo / jnp.sum(expo, axis=-1, keepdims=True)).astype(jnp.bfloat16)
                context.append(
                    jnp.dot(weight, values[:, cols], preferred_element_type=jnp.float32)
                    .astype(jnp.bfloat16)
                )
        context = jnp.concatenate(context, axis=1)
        live = live_ref[state_ref[1]] > 0.0
        for j in range(4):
            for b in range(4):
                load_out(j, b).wait()
        for b in range(4):
            term = jnp.dot(context, buf_out[b], preferred_element_type=jnp.float32)
            term = jnp.where(live, term, 0.0).astype(keep_ref.dtype)
            cols = slice(b * width, (b + 1) * width)
            keep_ref[:, cols] = term[:HALF]
            send_ref[:, cols] = term[HALF:]


def run_layer(state, mine, other, gain, biases, lives, weights):
    rows, model = mine.shape
    width = weights[0].shape[1]
    vmem = pl.BlockSpec(memory_space=pltpu.VMEM)
    anywhere = pl.BlockSpec(memory_space=pl.ANY)
    half = jax.ShapeDtypeStruct((rows, model), jnp.bfloat16)
    return pl.pallas_call(
        layer_kernel,
        out_shape=(half, half),
        in_specs=[pl.BlockSpec(memory_space=pltpu.SMEM)] + [vmem] * 5 + [anywhere] * 5,
        out_specs=(vmem, vmem),
        scratch_shapes=[
            pltpu.VMEM((4, 3, model, width), jnp.bfloat16),
            pltpu.VMEM((4, 4 * width, width), jnp.bfloat16),
            pltpu.SemaphoreType.DMA((4, 3)),
            pltpu.SemaphoreType.DMA((4, 4)),
        ],
        compiler_params=pltpu.CompilerParams(vmem_limit_bytes=56 * 1024 * 1024),
        cost_estimate=pl.CostEstimate(
            flops=2 * WINDOW * model * width * 16, bytes_accessed=16 * model * width * 2,
            transcendentals=WINDOW * WINDOW * 8,
        ),
    )(state, mine, other, gain, biases, lives, *weights)


def group_bounds(segments):
    seq_len = segments.shape[0]
    quarter = seq_len // SIDE
    position = jnp.arange(seq_len, dtype=jnp.int32)
    before = jnp.concatenate([segments[:1] - 1, segments[:-1]])
    begins = segments != before
    bounds = [jnp.int32(0)]
    for g in range(1, SIDE):
        middle = g * quarter
        low = jnp.max(jnp.where(begins & (position <= middle), position, 0))
        high = jnp.min(jnp.where(begins & (position >= middle), position, seq_len))
        bounds.append(jnp.where(middle - low <= high - middle, low, high))
    return jnp.stack(bounds)


def window_masks(segments, prefixes, length, start, core):
    seq_len = segments.shape[0]
    count_seg = prefixes.shape[0]
    position = jnp.arange(seq_len, dtype=jnp.int32)
    member = segments[:, None] == jnp.arange(count_seg, dtype=jnp.int32)[None, :]
    seg_start = jnp.min(jnp.where(member, position[:, None], jnp.int32(seq_len)), axis=0)
    prefix_end = jnp.sum(jnp.where(member, (seg_start + prefixes)[None, :], jnp.int32(0)), axis=1)

    def halves_of(array):
        return jnp.concatenate([
            lax.dynamic_slice_in_dim(array, start + HALF * core, HALF, 0),
            lax.dynamic_slice_in_dim(array, start + HALF * (1 - core), HALF, 0),
        ])

    seg_w, end_w, pos_w = halves_of(segments), halves_of(prefix_end), halves_of(position)
    key_ok = (pos_w[None, :] <= pos_w[:, None]) | (pos_w[None, :] < end_w[None, :])
    live_keys = (pos_w[None, :] < length) | (pos_w[None, :] == pos_w[:, None])
    visible = (seg_w[:, None] == seg_w[None, :]) & key_ok & live_keys
    bias = jnp.where(visible, jnp.float32(0.0), jnp.float32(-1e30))
    live = (pos_w < length).astype(jnp.float32)[:, None]
    return bias, live


def shards(
    inputs, norm_gain, w_query, w_key, w_value, w_output, segment_ids, prefix_lengths, batch_lengths
):
    section = lax.axis_index("section")
    sections = lax.axis_size("section")
    groups = lax.axis_size("dp")
    place = lax.axis_index("dp")
    micro_count, row_count, model = inputs.shape
    seq_len = row_count * groups
    quarter = seq_len // SIDE
    planes = sections // 2
    plane, core = section // 2, section % 2
    y, x = place // SIDE, place % SIDE
    group, member = (y // 2) * 2 + x // 2, (y % 2) * 2 + x % 2
    start = jnp.asarray(STARTS, jnp.int32)[group]

    def move(value, where):
        pairs = []
        for s in range(sections):
            for a in range(SIDE):
                for b in range(SIDE):
                    to, ta, tb = where(s, a, b)
                    pairs.append((
                        s * groups + a * SIDE + b,
                        (to % sections) * groups + (ta % SIDE) * SIDE + tb % SIDE,
                    ))
        return lax.ppermute(value, AXES, pairs)

    def swap_cores(value):
        return move(value, lambda s, a, b: (s ^ 1, a, b))

    def pack(h):
        width = w_query.shape[2] // 2
        cols = slice(h * width, (h + 1) * width)
        rows = w_output[0, cols]
        blocks = [rows[:, b * width : (b + 1) * width] for b in range(model // width)]
        return jnp.concatenate(
            [w_query[0, :, cols], w_key[0, :, cols], w_value[0, :, cols]] + blocks, axis=0
        )

    first = core == 0
    low, high = pack(0), pack(1)
    kept = jnp.where(first, low, high)
    got = swap_cores(jnp.where(first, high, low))
    got_gain = swap_cores(norm_gain)
    gain_a, gain_b = jnp.where(first, norm_gain, got_gain), jnp.where(first, got_gain, norm_gain)

    def gather(weights):
        def over_x(value):
            return move(value, lambda s, a, b: (s, a, b ^ 3))

        def over_y(value):
            return move(value, lambda s, a, b: (s, a ^ 3, b))

        cut = weights.shape[0] // 2
        from_x, from_y = over_x(weights), over_y(weights)
        return [weights, from_x, from_y, over_y(from_x[:cut]), over_x(from_y[cut:])]

    weights_a = gather(jnp.where(first, kept, got))
    before_b = jnp.where(first, got, kept)
    before_b, weights_a[3], weights_a[4] = lax.optimization_barrier(
        (before_b, weights_a[3], weights_a[4])
    )
    weights_b = gather(before_b)

    inputs_all = lax.all_gather(inputs, "dp", axis=1, tiled=True)
    window_mine = lax.dynamic_slice_in_dim(inputs_all, start + HALF * core, HALF, 1)
    window_other = lax.dynamic_slice_in_dim(inputs_all, start + HALF * (1 - core), HALF, 1)

    masks = [
        window_masks(segment_ids[m], prefix_lengths[m], batch_lengths[m], start, core)
        for m in range(micro_count)
    ]
    biases = jnp.stack([m[0] for m in masks])
    lives = jnp.stack([m[1] for m in masks])

    def one_layer(state, mine, other, gain, weights):
        keep, send = run_layer(state, mine, other, gain, biases, lives, weights)
        chip = (
            keep.astype(jnp.float32) + swap_cores(send).astype(jnp.float32)
        ).astype(jnp.bfloat16)
        total = mine.astype(jnp.float32) + chip.astype(jnp.float32)
        for piece in (
            move(chip, lambda s, a, b: (s, a ^ 1, b ^ 1)),
            move(chip, lambda s, a, b: (s, a ^ 1, b)),
            move(chip, lambda s, a, b: (s, a, b ^ 1)),
        ):
            total = total + piece.astype(jnp.float32)
        return total.astype(jnp.bfloat16)

    def one_round(turn, carry, last=False):
        mine, other, stash = carry
        micro = turn - plane
        active = (micro >= 0) & (micro < micro_count)
        micro = jnp.clip(micro, 0, micro_count - 1)
        state = jnp.stack([active.astype(jnp.int32), micro.astype(jnp.int32)])
        out_a = one_layer(state, mine, other, gain_a, weights_a)
        out_b = one_layer(state, out_a, swap_cores(out_a), gain_b, weights_b)
        stash = [
            [jnp.where(active & (micro == m), new, stash[n][m]) for m in range(micro_count)]
            for n, new in enumerate((out_a, out_b))
        ]
        if not last:
            onward = jnp.where(plane == planes - 1, window_mine[1], out_b)
            mine = move(onward, lambda s, a, b: (s + 2, a, b))
            other = swap_cores(mine)
        return mine, other, stash

    blank = jnp.zeros((HALF, model), jnp.bfloat16)
    carry = (window_mine[0], window_other[0], [[blank] * micro_count] * 2)
    carry = one_round(jnp.int32(0), carry)
    turns = planes + micro_count - 1
    carry = lax.fori_loop(1, turns - 1, one_round, carry)
    _, _, stash = one_round(jnp.int32(turns - 1), carry, last=True)

    stash_a, stash_b = jnp.stack(stash[0]), jnp.stack(stash[1])
    whole = jnp.concatenate(
        [jnp.where(first, stash_a, stash_b), swap_cores(jnp.where(first, stash_b, stash_a))], axis=1
    )

    def block_at(slot):
        local = (slot - start + HALF * core) % WINDOW
        return lax.dynamic_slice_in_dim(whole, local, row_count, 1)

    def owner(s, a, b, shift):
        g, t = (a // 2) * 2 + b // 2, (a % 2) * 2 + b % 2
        return (s, g + (0 if not shift else 1 if t < SIDE // 2 else -1), t)

    side = jnp.where(member < SIDE // 2, group + 1, group - 1)
    mine = move(block_at(quarter * group + row_count * member),
                lambda s, a, b: owner(s, a, b, False))
    other = move(block_at(quarter * side + row_count * member),
                 lambda s, a, b: owner(s, a, b, True))
    slots = place * row_count + jnp.arange(row_count, dtype=jnp.int32)
    picked = []
    for m in range(micro_count):
        bounds = group_bounds(segment_ids[m])
        holder = jnp.sum((slots[:, None] >= bounds[None, 1:]).astype(jnp.int32), axis=1)
        picked.append(jnp.where((holder == y)[:, None], mine[m], other[m]))
    return jnp.stack(picked)[None]


def solution(mesh):
    return jax.shard_map(
        shards,
        mesh=mesh,
        in_specs=(
            P(None, "dp", None),
            P("section", None),
            P("section", None, "dp"),
            P("section", None, "dp"),
            P("section", None, "dp"),
            P("section", "dp", None),
            P(),
            P(),
            P(),
        ),
        out_specs=P("section", None, "dp", None),
        check_vma=False,
    )
```

```python
import functools

import jax
import jax.numpy as jnp
from jax import lax
from jax.experimental import pallas as pl
from jax.experimental.pallas import tpu as pltpu
from jax.sharding import PartitionSpec as P

DH = 128
SIDE = 4
WINDOW = 128
HALF = WINDOW // 2
STARTS = (0, 32, 96, 128)
AXES = ("section", "dp")


def layer_kernel(turn, place_ref, mine_ref, other_ref, gain_ref, bias_ref, *refs):
    own, from_x, from_y, top, bottom = refs[:5]
    keep_ref, send_ref = refs[5:]
    model, width = mine_ref.shape[1], own.shape[1]
    plane, core, start = place_ref[0], place_ref[1], place_ref[2]
    micro = turn - plane

    def weight(j, n, row, rows):
        if j < 3:
            return (own, from_x, from_y)[j][pl.ds(n * model + row, rows)]
        return (top if n < 2 else bottom)[pl.ds((n % 2) * model + row, rows)]

    @pl.when((micro >= 0) & (micro < bias_ref.shape[0]))
    def _():
        wide = jnp.concatenate([mine_ref[...], other_ref[...]], axis=0).astype(jnp.float32)
        mean_square = jnp.mean(wide * wide, axis=-1, keepdims=True)
        normed = (wide * lax.rsqrt(mean_square + 1e-06) * gain_ref[...]).astype(jnp.bfloat16)
        bias = bias_ref[micro]
        context = []
        for j in range(4):
            queries, keyed, values = [
                jnp.dot(
                    normed, weight(j, n, 0, model), preferred_element_type=jnp.float32
                ).astype(jnp.bfloat16)
                for n in range(3)
            ]
            for head in range(width // DH):
                cols = slice(head * DH, (head + 1) * DH)
                scores = lax.dot_general(
                    queries[:, cols], keyed[:, cols], (((1,), (1,)), ((), ())),
                    preferred_element_type=jnp.float32,
                ) * DH ** (-0.5) + bias
                expo = jnp.exp(scores - jnp.max(scores, axis=-1, keepdims=True))
                share = (expo / jnp.sum(expo, axis=-1, keepdims=True)).astype(jnp.bfloat16)
                context.append(
                    jnp.dot(share, values[:, cols], preferred_element_type=jnp.float32)
                    .astype(jnp.bfloat16)
                )
        heads = width // DH
        context = [
            jnp.concatenate(context[j * heads : (j + 1) * heads], axis=1) for j in range(4)
        ]
        row = lax.broadcasted_iota(jnp.int32, (WINDOW, width), 0)
        slot = start + (row + HALF * core) % WINDOW
        live = slot < place_ref[3 + micro]
        for b in range(model // width):
            term = sum(
                jnp.dot(
                    context[j], weight(j, 3, b * width, width), preferred_element_type=jnp.float32
                )
                for j in range(4)
            )
            term = jnp.where(live, term, 0.0).astype(keep_ref.dtype)
            cols = slice(b * width, (b + 1) * width)
            keep_ref[:, cols] = term[:HALF]
            send_ref[:, cols] = term[HALF:]


def run_layer(turn, place, mine, other, gain, biases, weights):
    rows, model = mine.shape
    width = weights[0].shape[1]
    vmem = pl.BlockSpec(memory_space=pltpu.VMEM)
    half = jax.ShapeDtypeStruct((rows, model), jnp.bfloat16)
    resident = [pltpu.with_memory_space_constraint(v, pltpu.VMEM) for v in [biases] + weights]
    return pl.pallas_call(
        functools.partial(layer_kernel, turn),
        out_shape=(half, half),
        in_specs=[pl.BlockSpec(memory_space=pltpu.SMEM)] + [vmem] * 9,
        out_specs=(vmem, vmem),
        compiler_params=pltpu.CompilerParams(vmem_limit_bytes=16 * 1024 * 1024),
        cost_estimate=pl.CostEstimate(
            flops=2 * WINDOW * model * width * 16, bytes_accessed=16 * model * width * 2,
            transcendentals=WINDOW * WINDOW * 8,
        ),
    )(place, mine, other, gain, *resident)


def group_bounds(segments):
    seq_len = segments.shape[0]
    quarter = seq_len // SIDE
    position = jnp.arange(seq_len, dtype=jnp.int32)
    before = jnp.concatenate([segments[:1] - 1, segments[:-1]])
    begins = segments != before
    bounds = [jnp.int32(0)]
    for g in range(1, SIDE):
        middle = g * quarter
        low = jnp.max(jnp.where(begins & (position <= middle), position, 0))
        high = jnp.min(jnp.where(begins & (position >= middle), position, seq_len))
        bounds.append(jnp.where(middle - low <= high - middle, low, high))
    return jnp.stack(bounds)


def window_masks(segments, prefixes, length, start, core):
    seq_len = segments.shape[0]
    count_seg = prefixes.shape[0]
    position = jnp.arange(seq_len, dtype=jnp.int32)
    member = segments[:, None] == jnp.arange(count_seg, dtype=jnp.int32)[None, :]
    seg_start = jnp.min(jnp.where(member, position[:, None], jnp.int32(seq_len)), axis=0)
    prefix_end = jnp.sum(jnp.where(member, (seg_start + prefixes)[None, :], jnp.int32(0)), axis=1)

    def halves_of(array):
        return jnp.concatenate([
            lax.dynamic_slice_in_dim(array, start + HALF * core, HALF, 0),
            lax.dynamic_slice_in_dim(array, start + HALF * (1 - core), HALF, 0),
        ])

    seg_w, end_w, pos_w = halves_of(segments), halves_of(prefix_end), halves_of(position)
    key_ok = (pos_w[None, :] <= pos_w[:, None]) | (pos_w[None, :] < end_w[None, :])
    live_keys = (pos_w[None, :] < length) | (pos_w[None, :] == pos_w[:, None])
    visible = (seg_w[:, None] == seg_w[None, :]) & key_ok & live_keys
    return jnp.where(visible, jnp.float32(0.0), jnp.float32(-1e30))


def shards(
    inputs, norm_gain, w_query, w_key, w_value, w_output, segment_ids, prefix_lengths, batch_lengths
):
    section = lax.axis_index("section")
    sections = lax.axis_size("section")
    groups = lax.axis_size("dp")
    place = lax.axis_index("dp")
    micro_count, row_count, model = inputs.shape
    seq_len = row_count * groups
    quarter = seq_len // SIDE
    planes = sections // 2
    plane, core = section // 2, section % 2
    y, x = place // SIDE, place % SIDE
    group, member = (y // 2) * 2 + x // 2, (y % 2) * 2 + x % 2
    start = jnp.asarray(STARTS, jnp.int32)[group]

    def move(value, where):
        pairs = []
        for s in range(sections):
            for a in range(SIDE):
                for b in range(SIDE):
                    to, ta, tb = where(s, a, b)
                    pairs.append((
                        s * groups + a * SIDE + b,
                        (to % sections) * groups + (ta % SIDE) * SIDE + tb % SIDE,
                    ))
        return lax.ppermute(value, AXES, pairs)

    def swap_cores(value):
        return move(value, lambda s, a, b: (s ^ 1, a, b))

    def pack(h):
        width = w_query.shape[2] // 2
        cols = slice(h * width, (h + 1) * width)
        rows = w_output[0, cols]
        blocks = [rows[:, b * width : (b + 1) * width] for b in range(model // width)]
        return jnp.concatenate(
            [w_query[0, :, cols], w_key[0, :, cols], w_value[0, :, cols]] + blocks, axis=0
        )

    first = core == 0
    low, high = pack(0), pack(1)
    kept = jnp.where(first, low, high)
    got = swap_cores(jnp.where(first, high, low))
    got_gain = swap_cores(norm_gain)
    gain_a, gain_b = jnp.where(first, norm_gain, got_gain), jnp.where(first, got_gain, norm_gain)

    def over_x(value):
        return move(value, lambda s, a, b: (s, a, b ^ 3))

    def over_y(value):
        return move(value, lambda s, a, b: (s, a ^ 3, b))

    cut = low.shape[0] // 2
    own_a, own_b = jnp.where(first, kept, got), jnp.where(first, got, kept)
    x_a, y_a = over_x(own_a), over_y(own_a)
    weights_a = [own_a, x_a, y_a, over_y(x_a[:cut]), over_x(y_a[cut:])]
    own_b, weights_a[3], weights_a[4] = lax.optimization_barrier(
        (own_b, weights_a[3], weights_a[4])
    )
    x_b, y_b = over_x(own_b), over_y(own_b)

    inputs_all = lax.all_gather(inputs, "dp", axis=1, tiled=True)
    window_mine = lax.dynamic_slice_in_dim(inputs_all, start + HALF * core, HALF, 1)
    window_other = lax.dynamic_slice_in_dim(inputs_all, start + HALF * (1 - core), HALF, 1)

    biases = jnp.stack([
        window_masks(segment_ids[m], prefix_lengths[m], batch_lengths[m], start, core)
        for m in range(micro_count)
    ])
    where_am_i = jnp.concatenate([
        jnp.stack([plane, core, start]).astype(jnp.int32), batch_lengths.astype(jnp.int32)
    ])

    def one_layer(turn, mine, other, gain, weights):
        keep, send = run_layer(turn, where_am_i, mine, other, gain, biases, weights)
        chip = (
            keep.astype(jnp.float32) + swap_cores(send).astype(jnp.float32)
        ).astype(jnp.bfloat16)
        total = mine.astype(jnp.float32) + chip.astype(jnp.float32)
        for piece in (
            move(chip, lambda s, a, b: (s, a ^ 1, b ^ 1)),
            move(chip, lambda s, a, b: (s, a ^ 1, b)),
            move(chip, lambda s, a, b: (s, a, b ^ 1)),
        ):
            total = total + piece.astype(jnp.float32)
        return total.astype(jnp.bfloat16)

    side = jnp.where(member < SIDE // 2, group + 1, group - 1)
    own_at = (quarter * group + row_count * member - start) % WINDOW
    side_at = (quarter * side + row_count * member - start) % WINDOW

    def blocks(rows):
        return jnp.stack([
            lax.dynamic_slice_in_dim(rows, at % HALF, row_count, 0) for at in (own_at, side_at)
        ])

    blank = jnp.zeros((2, row_count, model), jnp.bfloat16)
    stash = [[blank] * micro_count, [blank] * micro_count]

    def keep_blocks(layer, turn, rows):
        found = blocks(rows)
        for m in range(micro_count):
            if 0 <= turn - m < planes:
                stash[layer][m] = jnp.where(plane == turn - m, found, stash[layer][m])

    mine, other = window_mine[0], window_other[0]
    weights_b = None
    turns = planes + micro_count - 1
    for turn in range(turns):
        out_a = one_layer(turn, mine, other, gain_a, weights_a)
        if weights_b is None:
            x_b, y_b, out_a = lax.optimization_barrier((x_b, y_b, out_a))
            weights_b = [own_b, x_b, y_b, over_y(x_b[:cut]), over_x(y_b[cut:])]
        out_b = one_layer(turn, out_a, swap_cores(out_a), gain_b, weights_b)
        if turn < turns - 1:
            onward = (
                jnp.where(plane == planes - 1, window_mine[1], out_b) if turn == 0 else out_b
            )
            mine = move(onward, lambda s, a, b: (s + 2, a, b))
            other = swap_cores(mine)
        keep_blocks(0, turn, out_a)
        keep_blocks(1, turn, out_b)

    stash_a, stash_b = [jnp.stack(rows, axis=1) for rows in stash]
    here = jnp.where(first, stash_a, stash_b)
    there = swap_cores(jnp.where(first, stash_b, stash_a))

    def owner(s, a, b, shift):
        g, t = (a // 2) * 2 + b // 2, (a % 2) * 2 + b % 2
        return (s, g + (0 if not shift else 1 if t < SIDE // 2 else -1), t)

    mine = move(jnp.where(own_at // HALF == core, here[0], there[0]),
                lambda s, a, b: owner(s, a, b, False))
    other = move(jnp.where(side_at // HALF == core, here[1], there[1]),
                 lambda s, a, b: owner(s, a, b, True))
    slots = place * row_count + jnp.arange(row_count, dtype=jnp.int32)
    picked = []
    for m in range(micro_count):
        bounds = group_bounds(segment_ids[m])
        holder = jnp.sum((slots[:, None] >= bounds[None, 1:]).astype(jnp.int32), axis=1)
        picked.append(jnp.where((holder == y)[:, None], mine[m], other[m]))
    return jnp.stack(picked)[None]


def solution(mesh):
    return jax.shard_map(
        shards,
        mesh=mesh,
        in_specs=(
            P(None, "dp", None),
            P("section", None),
            P("section", None, "dp"),
            P("section", None, "dp"),
            P("section", None, "dp"),
            P("section", "dp", None),
            P(),
            P(),
            P(),
        ),
        out_specs=P("section", None, "dp", None),
        check_vma=False,
    )
```

```python
import functools

import jax
import jax.numpy as jnp
from jax import lax
from jax.experimental import pallas as pl
from jax.experimental.pallas import tpu as pltpu
from jax.sharding import PartitionSpec as P

DH = 128
SIDE = 4
WINDOW = 128
HALF = WINDOW // 2
STARTS = (0, 32, 96, 128)
AXES = ("section", "dp")


def layer_kernel(turn, place_ref, mine_ref, other_ref, gain_ref, bias_ref, *refs):
    own, from_x, from_y, top, bottom = refs[:5]
    keep_ref, send_ref = refs[5:]
    model, width = mine_ref.shape[1], own.shape[1]
    plane, core, start = place_ref[0], place_ref[1], place_ref[2]
    micro = turn - plane

    def weight(j, n, row, rows):
        if j < 3:
            return (own, from_x, from_y)[j][pl.ds(n * model + row, rows)]
        return (top if n < 2 else bottom)[pl.ds((n % 2) * model + row, rows)]

    @pl.when((micro >= 0) & (micro < bias_ref.shape[0]))
    def _():
        wide = jnp.concatenate([mine_ref[...], other_ref[...]], axis=0).astype(jnp.float32)
        mean_square = jnp.mean(wide * wide, axis=-1, keepdims=True)
        normed = (wide * lax.rsqrt(mean_square + 1e-06) * gain_ref[...]).astype(jnp.bfloat16)
        bias = bias_ref[micro]
        context = []
        for j in range(4):
            queries, keyed, values = [
                jnp.dot(
                    normed, weight(j, n, 0, model), preferred_element_type=jnp.float32
                ).astype(jnp.bfloat16)
                for n in range(3)
            ]
            for head in range(width // DH):
                cols = slice(head * DH, (head + 1) * DH)
                scores = lax.dot_general(
                    queries[:, cols], keyed[:, cols], (((1,), (1,)), ((), ())),
                    preferred_element_type=jnp.float32,
                ) * DH ** (-0.5) + bias
                expo = jnp.exp(scores - jnp.max(scores, axis=-1, keepdims=True))
                share = (expo / jnp.sum(expo, axis=-1, keepdims=True)).astype(jnp.bfloat16)
                context.append(
                    jnp.dot(share, values[:, cols], preferred_element_type=jnp.float32)
                    .astype(jnp.bfloat16)
                )
        heads = width // DH
        context = [
            jnp.concatenate(context[j * heads : (j + 1) * heads], axis=1) for j in range(4)
        ]
        row = lax.broadcasted_iota(jnp.int32, (WINDOW, width), 0)
        slot = start + (row + HALF * core) % WINDOW
        live = slot < place_ref[3 + micro]
        for b in range(model // width):
            term = sum(
                jnp.dot(
                    context[j], weight(j, 3, b * width, width), preferred_element_type=jnp.float32
                )
                for j in range(4)
            )
            term = jnp.where(live, term, 0.0).astype(keep_ref.dtype)
            cols = slice(b * width, (b + 1) * width)
            keep_ref[:, cols] = term[:HALF]
            send_ref[:, cols] = term[HALF:]


def run_layer(turn, place, mine, other, gain, biases, weights):
    rows, model = mine.shape
    width = weights[0].shape[1]
    vmem = pl.BlockSpec(memory_space=pltpu.VMEM)
    half = jax.ShapeDtypeStruct((rows, model), jnp.bfloat16)
    resident = [pltpu.with_memory_space_constraint(v, pltpu.VMEM) for v in [biases] + weights]
    return pl.pallas_call(
        functools.partial(layer_kernel, turn),
        out_shape=(half, half),
        in_specs=[pl.BlockSpec(memory_space=pltpu.SMEM)] + [vmem] * 9,
        out_specs=(vmem, vmem),
        compiler_params=pltpu.CompilerParams(vmem_limit_bytes=16 * 1024 * 1024),
        cost_estimate=pl.CostEstimate(
            flops=2 * WINDOW * model * width * 16, bytes_accessed=16 * model * width * 2,
            transcendentals=WINDOW * WINDOW * 8,
        ),
    )(place, mine, other, gain, *resident)


def group_bounds(segments):
    seq_len = segments.shape[0]
    quarter = seq_len // SIDE
    position = jnp.arange(seq_len, dtype=jnp.int32)
    before = jnp.concatenate([segments[:1] - 1, segments[:-1]])
    begins = segments != before
    bounds = [jnp.int32(0)]
    for g in range(1, SIDE):
        middle = g * quarter
        low = jnp.max(jnp.where(begins & (position <= middle), position, 0))
        high = jnp.min(jnp.where(begins & (position >= middle), position, seq_len))
        bounds.append(jnp.where(middle - low <= high - middle, low, high))
    return jnp.stack(bounds)


def window_masks(segments, prefixes, length, start, core):
    seq_len = segments.shape[0]
    count_seg = prefixes.shape[0]
    position = jnp.arange(seq_len, dtype=jnp.int32)
    member = segments[:, None] == jnp.arange(count_seg, dtype=jnp.int32)[None, :]
    seg_start = jnp.min(jnp.where(member, position[:, None], jnp.int32(seq_len)), axis=0)
    prefix_end = jnp.sum(jnp.where(member, (seg_start + prefixes)[None, :], jnp.int32(0)), axis=1)

    def halves_of(array):
        return jnp.concatenate([
            lax.dynamic_slice_in_dim(array, start + HALF * core, HALF, 0),
            lax.dynamic_slice_in_dim(array, start + HALF * (1 - core), HALF, 0),
        ])

    seg_w, end_w, pos_w = halves_of(segments), halves_of(prefix_end), halves_of(position)
    key_ok = (pos_w[None, :] <= pos_w[:, None]) | (pos_w[None, :] < end_w[None, :])
    live_keys = (pos_w[None, :] < length) | (pos_w[None, :] == pos_w[:, None])
    visible = (seg_w[:, None] == seg_w[None, :]) & key_ok & live_keys
    return jnp.where(visible, jnp.float32(0.0), jnp.float32(-1e30))


def shards(
    inputs, norm_gain, w_query, w_key, w_value, w_output, segment_ids, prefix_lengths, batch_lengths
):
    section = lax.axis_index("section")
    sections = lax.axis_size("section")
    groups = lax.axis_size("dp")
    place = lax.axis_index("dp")
    micro_count, row_count, model = inputs.shape
    seq_len = row_count * groups
    quarter = seq_len // SIDE
    planes = sections // 2
    plane, core = section // 2, section % 2
    y, x = place // SIDE, place % SIDE
    group, member = (y // 2) * 2 + x // 2, (y % 2) * 2 + x % 2
    start = jnp.asarray(STARTS, jnp.int32)[group]

    def move(value, where):
        pairs = []
        for s in range(sections):
            for a in range(SIDE):
                for b in range(SIDE):
                    to, ta, tb = where(s, a, b)
                    pairs.append((
                        s * groups + a * SIDE + b,
                        (to % sections) * groups + (ta % SIDE) * SIDE + tb % SIDE,
                    ))
        return lax.ppermute(value, AXES, pairs)

    def swap_cores(value):
        return move(value, lambda s, a, b: (s ^ 1, a, b))

    def pack(h):
        width = w_query.shape[2] // 2
        cols = slice(h * width, (h + 1) * width)
        rows = w_output[0, cols]
        blocks = [rows[:, b * width : (b + 1) * width] for b in range(model // width)]
        return jnp.concatenate(
            [w_query[0, :, cols], w_key[0, :, cols], w_value[0, :, cols]] + blocks, axis=0
        )

    first = core == 0
    low, high = pack(0), pack(1)
    kept = jnp.where(first, low, high)
    got = swap_cores(jnp.where(first, high, low))
    got_gain = swap_cores(norm_gain)
    gain_a, gain_b = jnp.where(first, norm_gain, got_gain), jnp.where(first, got_gain, norm_gain)

    def over_x(value):
        return move(value, lambda s, a, b: (s, a, b ^ 3))

    def over_y(value):
        return move(value, lambda s, a, b: (s, a ^ 3, b))

    cut = low.shape[0] // 2
    own_a, own_b = jnp.where(first, kept, got), jnp.where(first, got, kept)
    x_a, y_a = over_x(own_a), over_y(own_a)
    own_b, x_a, y_a = lax.optimization_barrier((own_b, x_a, y_a))
    weights_a = [own_a, x_a, y_a, over_y(x_a[:cut]), over_x(y_a[cut:])]
    x_b, y_b = over_x(own_b), over_y(own_b)
    weights_b = [own_b, x_b, y_b, over_y(x_b[:cut]), over_x(y_b[cut:])]

    inputs_all = lax.all_gather(inputs, "dp", axis=1, tiled=True)
    window_mine = lax.dynamic_slice_in_dim(inputs_all, start + HALF * core, HALF, 1)
    window_other = lax.dynamic_slice_in_dim(inputs_all, start + HALF * (1 - core), HALF, 1)

    biases = jnp.stack([
        window_masks(segment_ids[m], prefix_lengths[m], batch_lengths[m], start, core)
        for m in range(micro_count)
    ])
    where_am_i = jnp.concatenate([
        jnp.stack([plane, core, start]).astype(jnp.int32), batch_lengths.astype(jnp.int32)
    ])

    def across(s, a, b, along_y):
        return (s, a ^ 1, b) if along_y else (s, a, b ^ 1)

    def one_layer(turn, mine, other, gain, weights):
        keep, send = run_layer(turn, where_am_i, mine, other, gain, biases, weights)
        chip = (
            keep.astype(jnp.float32) + swap_cores(send).astype(jnp.float32)
        ).astype(jnp.bfloat16)
        pair = (
            chip.astype(jnp.float32)
            + move(chip, lambda s, a, b: across(s, a, b, s % 2)).astype(jnp.float32)
        ).astype(jnp.bfloat16)
        total = (
            mine.astype(jnp.float32)
            + pair.astype(jnp.float32)
            + move(pair, lambda s, a, b: across(s, a, b, 1 - s % 2)).astype(jnp.float32)
        )
        return total.astype(jnp.bfloat16)

    side = jnp.where(member < SIDE // 2, group + 1, group - 1)
    own_at = (quarter * group + row_count * member - start) % WINDOW
    side_at = (quarter * side + row_count * member - start) % WINDOW

    def blocks(rows):
        return jnp.stack([
            lax.dynamic_slice_in_dim(rows, at % HALF, row_count, 0) for at in (own_at, side_at)
        ])

    blank = jnp.zeros((2, row_count, model), jnp.bfloat16)
    stash = [[blank] * micro_count, [blank] * micro_count]

    def keep_blocks(layer, turn, rows):
        found = blocks(rows)
        for m in range(micro_count):
            if 0 <= turn - m < planes:
                stash[layer][m] = jnp.where(plane == turn - m, found, stash[layer][m])

    mine, other = window_mine[0], window_other[0]
    turns = planes + micro_count - 1
    for turn in range(turns):
        out_a = one_layer(turn, mine, other, gain_a, weights_a)
        out_b = one_layer(turn, out_a, swap_cores(out_a), gain_b, weights_b)
        if turn < turns - 1:
            onward = (
                jnp.where(plane == planes - 1, window_mine[1], out_b) if turn == 0 else out_b
            )
            mine = move(onward, lambda s, a, b: (s + 2, a, b))
            other = swap_cores(mine)
        keep_blocks(0, turn, out_a)
        keep_blocks(1, turn, out_b)

    stash_a, stash_b = [jnp.stack(rows, axis=1) for rows in stash]
    here = jnp.where(first, stash_a, stash_b)
    there = swap_cores(jnp.where(first, stash_b, stash_a))

    def owner(s, a, b, shift):
        g, t = (a // 2) * 2 + b // 2, (a % 2) * 2 + b % 2
        return (s, g + (0 if not shift else 1 if t < SIDE // 2 else -1), t)

    mine = move(jnp.where(own_at // HALF == core, here[0], there[0]),
                lambda s, a, b: owner(s, a, b, False))
    other = move(jnp.where(side_at // HALF == core, here[1], there[1]),
                 lambda s, a, b: owner(s, a, b, True))
    slots = place * row_count + jnp.arange(row_count, dtype=jnp.int32)
    picked = []
    for m in range(micro_count):
        bounds = group_bounds(segment_ids[m])
        holder = jnp.sum((slots[:, None] >= bounds[None, 1:]).astype(jnp.int32), axis=1)
        picked.append(jnp.where((holder == y)[:, None], mine[m], other[m]))
    return jnp.stack(picked)[None]


def solution(mesh):
    return jax.shard_map(
        shards,
        mesh=mesh,
        in_specs=(
            P(None, "dp", None),
            P("section", None),
            P("section", None, "dp"),
            P("section", None, "dp"),
            P("section", None, "dp"),
            P("section", "dp", None),
            P(),
            P(),
            P(),
        ),
        out_specs=P("section", None, "dp", None),
        check_vma=False,
    )
```

```python
import functools

import jax
import jax.numpy as jnp
from jax import lax
from jax.experimental import pallas as pl
from jax.experimental.pallas import tpu as pltpu
from jax.sharding import PartitionSpec as P

DH = 128
SIDE = 4
WINDOW = 128
HALF = WINDOW // 2
STARTS = (0, 32, 96, 128)
AXES = ("section", "dp")


def layer_kernel(turn, place_ref, mine_ref, other_ref, gain_ref, bias_ref, *refs):
    weights, (keep_ref, send_ref) = refs[:8], refs[8:]
    model, width = mine_ref.shape[1], weights[0].shape[1]
    plane, core, start = place_ref[0], place_ref[1], place_ref[2]
    micro = turn - plane

    def weight(j, n, row, rows):
        return weights[2 * j + n // 2][pl.ds((n % 2) * model + row, rows)]

    @pl.when((micro >= 0) & (micro < bias_ref.shape[0]))
    def _():
        wide = jnp.concatenate([mine_ref[...], other_ref[...]], axis=0).astype(jnp.float32)
        mean_square = jnp.mean(wide * wide, axis=-1, keepdims=True)
        normed = (wide * lax.rsqrt(mean_square + 1e-06) * gain_ref[...]).astype(jnp.bfloat16)
        bias = bias_ref[micro]
        context = []
        for j in range(4):
            queries, keyed, values = [
                jnp.dot(
                    normed, weight(j, n, 0, model), preferred_element_type=jnp.float32
                ).astype(jnp.bfloat16)
                for n in range(3)
            ]
            for head in range(width // DH):
                cols = slice(head * DH, (head + 1) * DH)
                scores = lax.dot_general(
                    queries[:, cols], keyed[:, cols], (((1,), (1,)), ((), ())),
                    preferred_element_type=jnp.float32,
                ) * DH ** (-0.5) + bias
                expo = jnp.exp(scores - jnp.max(scores, axis=-1, keepdims=True))
                share = (expo / jnp.sum(expo, axis=-1, keepdims=True)).astype(jnp.bfloat16)
                context.append(
                    jnp.dot(share, values[:, cols], preferred_element_type=jnp.float32)
                    .astype(jnp.bfloat16)
                )
        heads = width // DH
        context = [
            jnp.concatenate(context[j * heads : (j + 1) * heads], axis=1) for j in range(4)
        ]
        row = lax.broadcasted_iota(jnp.int32, (WINDOW, width), 0)
        slot = start + (row + HALF * core) % WINDOW
        live = slot < place_ref[3 + micro]
        for b in range(model // width):
            term = sum(
                jnp.dot(
                    context[j], weight(j, 3, b * width, width), preferred_element_type=jnp.float32
                )
                for j in range(4)
            )
            term = jnp.where(live, term, 0.0).astype(keep_ref.dtype)
            cols = slice(b * width, (b + 1) * width)
            keep_ref[:, cols] = term[:HALF]
            send_ref[:, cols] = term[HALF:]


def run_layer(turn, place, mine, other, gain, biases, weights):
    rows, model = mine.shape
    width = weights[0].shape[1]
    vmem = pl.BlockSpec(memory_space=pltpu.VMEM)
    half = jax.ShapeDtypeStruct((rows, model), jnp.bfloat16)
    resident = [pltpu.with_memory_space_constraint(v, pltpu.VMEM) for v in [biases] + weights]
    return pl.pallas_call(
        functools.partial(layer_kernel, turn),
        out_shape=(half, half),
        in_specs=[pl.BlockSpec(memory_space=pltpu.SMEM)] + [vmem] * 12,
        out_specs=(vmem, vmem),
        compiler_params=pltpu.CompilerParams(vmem_limit_bytes=16 * 1024 * 1024),
        cost_estimate=pl.CostEstimate(
            flops=2 * WINDOW * model * width * 16, bytes_accessed=16 * model * width * 2,
            transcendentals=WINDOW * WINDOW * 8,
        ),
    )(place, mine, other, gain, *resident)


def group_bounds(segments):
    seq_len = segments.shape[0]
    quarter = seq_len // SIDE
    position = jnp.arange(seq_len, dtype=jnp.int32)
    before = jnp.concatenate([segments[:1] - 1, segments[:-1]])
    begins = segments != before
    bounds = [jnp.int32(0)]
    for g in range(1, SIDE):
        middle = g * quarter
        low = jnp.max(jnp.where(begins & (position <= middle), position, 0))
        high = jnp.min(jnp.where(begins & (position >= middle), position, seq_len))
        bounds.append(jnp.where(middle - low <= high - middle, low, high))
    return jnp.stack(bounds)


def window_masks(segments, prefixes, length, start, core):
    seq_len = segments.shape[0]
    count_seg = prefixes.shape[0]
    position = jnp.arange(seq_len, dtype=jnp.int32)
    member = segments[:, None] == jnp.arange(count_seg, dtype=jnp.int32)[None, :]
    seg_start = jnp.min(jnp.where(member, position[:, None], jnp.int32(seq_len)), axis=0)
    prefix_end = jnp.sum(jnp.where(member, (seg_start + prefixes)[None, :], jnp.int32(0)), axis=1)

    def halves_of(array):
        return jnp.concatenate([
            lax.dynamic_slice_in_dim(array, start + HALF * core, HALF, 0),
            lax.dynamic_slice_in_dim(array, start + HALF * (1 - core), HALF, 0),
        ])

    seg_w, end_w, pos_w = halves_of(segments), halves_of(prefix_end), halves_of(position)
    key_ok = (pos_w[None, :] <= pos_w[:, None]) | (pos_w[None, :] < end_w[None, :])
    live_keys = (pos_w[None, :] < length) | (pos_w[None, :] == pos_w[:, None])
    visible = (seg_w[:, None] == seg_w[None, :]) & key_ok & live_keys
    return jnp.where(visible, jnp.float32(0.0), jnp.float32(-1e30))


def shards(
    inputs, norm_gain, w_query, w_key, w_value, w_output, segment_ids, prefix_lengths, batch_lengths
):
    section = lax.axis_index("section")
    sections = lax.axis_size("section")
    groups = lax.axis_size("dp")
    place = lax.axis_index("dp")
    micro_count, row_count, model = inputs.shape
    seq_len = row_count * groups
    quarter = seq_len // SIDE
    planes = sections // 2
    plane, core = section // 2, section % 2
    y, x = place // SIDE, place % SIDE
    group, member = (y // 2) * 2 + x // 2, (y % 2) * 2 + x % 2
    start = jnp.asarray(STARTS, jnp.int32)[group]

    def move(value, where):
        pairs = []
        for s in range(sections):
            for a in range(SIDE):
                for b in range(SIDE):
                    to, ta, tb = where(s, a, b)
                    pairs.append((
                        s * groups + a * SIDE + b,
                        (to % sections) * groups + (ta % SIDE) * SIDE + tb % SIDE,
                    ))
        return lax.ppermute(value, AXES, pairs)

    def swap_cores(value):
        return move(value, lambda s, a, b: (s ^ 1, a, b))

    def pack(h):
        width = w_query.shape[2] // 2
        cols = slice(h * width, (h + 1) * width)
        rows = w_output[0, cols]
        blocks = [rows[:, b * width : (b + 1) * width] for b in range(model // width)]
        return (
            jnp.concatenate([w_query[0, :, cols], w_key[0, :, cols]], axis=0),
            jnp.concatenate([w_value[0, :, cols]] + blocks, axis=0),
        )

    first = core == 0
    low, high = pack(0), pack(1)
    kept = [jnp.where(first, p, q) for p, q in zip(low, high)]
    got = [swap_cores(jnp.where(first, q, p)) for p, q in zip(low, high)]
    got_gain = swap_cores(norm_gain)
    gain_a, gain_b = jnp.where(first, norm_gain, got_gain), jnp.where(first, got_gain, norm_gain)

    def over_x(value):
        return move(value, lambda s, a, b: (s, a, b ^ 3))

    def over_y(value):
        return move(value, lambda s, a, b: (s, a ^ 3, b))

    def gather(top, bottom):
        x_top, y_bottom = over_x(top), over_y(bottom)
        top, bottom, x_top, y_bottom = lax.optimization_barrier((top, bottom, x_top, y_bottom))
        far_top, far_bottom = over_y(x_top), over_x(y_bottom)
        y_top, x_bottom = over_y(top), over_x(bottom)
        return [top, bottom, x_top, x_bottom, y_top, y_bottom, far_top, far_bottom]

    weights_a = gather(*[jnp.where(first, p, q) for p, q in zip(kept, got)])
    own_b = [jnp.where(first, q, p) for p, q in zip(kept, got)]
    own_b, weights_a[6:] = lax.optimization_barrier((own_b, weights_a[6:]))
    weights_b = gather(*own_b)

    inputs_all = lax.all_gather(inputs, "dp", axis=1, tiled=True)
    window_mine = lax.dynamic_slice_in_dim(inputs_all, start + HALF * core, HALF, 1)
    window_other = lax.dynamic_slice_in_dim(inputs_all, start + HALF * (1 - core), HALF, 1)

    biases = jnp.stack([
        window_masks(segment_ids[m], prefix_lengths[m], batch_lengths[m], start, core)
        for m in range(micro_count)
    ])
    where_am_i = jnp.concatenate([
        jnp.stack([plane, core, start]).astype(jnp.int32), batch_lengths.astype(jnp.int32)
    ])

    def one_layer(turn, mine, other, gain, weights):
        keep, send = run_layer(turn, where_am_i, mine, other, gain, biases, weights)
        chip = (
            keep.astype(jnp.float32) + swap_cores(send).astype(jnp.float32)
        ).astype(jnp.bfloat16)
        total = mine.astype(jnp.float32) + chip.astype(jnp.float32)
        for piece in (
            move(chip, lambda s, a, b: (s, a ^ 1, b ^ 1)),
            move(chip, lambda s, a, b: (s, a ^ 1, b)),
            move(chip, lambda s, a, b: (s, a, b ^ 1)),
        ):
            total = total + piece.astype(jnp.float32)
        return total.astype(jnp.bfloat16)

    side = jnp.where(member < SIDE // 2, group + 1, group - 1)
    own_at = (quarter * group + row_count * member - start) % WINDOW
    side_at = (quarter * side + row_count * member - start) % WINDOW

    def blocks(rows):
        return jnp.stack([
            lax.dynamic_slice_in_dim(rows, at % HALF, row_count, 0) for at in (own_at, side_at)
        ])

    blank = jnp.zeros((2, row_count, model), jnp.bfloat16)
    stash = [[blank] * micro_count, [blank] * micro_count]

    def keep_blocks(layer, turn, rows):
        found = blocks(rows)
        for m in range(micro_count):
            if 0 <= turn - m < planes:
                stash[layer][m] = jnp.where(plane == turn - m, found, stash[layer][m])

    mine, other = window_mine[0], window_other[0]
    turns = planes + micro_count - 1
    for turn in range(turns):
        out_a = one_layer(turn, mine, other, gain_a, weights_a)
        out_b = one_layer(turn, out_a, swap_cores(out_a), gain_b, weights_b)
        if turn < turns - 1:
            onward = (
                jnp.where(plane == planes - 1, window_mine[1], out_b) if turn == 0 else out_b
            )
            mine = move(onward, lambda s, a, b: (s + 2, a, b))
            other = swap_cores(mine)
        keep_blocks(0, turn, out_a)
        keep_blocks(1, turn, out_b)

    stash_a, stash_b = [jnp.stack(rows, axis=1) for rows in stash]
    here = jnp.where(first, stash_a, stash_b)
    there = swap_cores(jnp.where(first, stash_b, stash_a))

    def owner(s, a, b, shift):
        g, t = (a // 2) * 2 + b // 2, (a % 2) * 2 + b % 2
        return (s, g + (0 if not shift else 1 if t < SIDE // 2 else -1), t)

    mine = move(jnp.where(own_at // HALF == core, here[0], there[0]),
                lambda s, a, b: owner(s, a, b, False))
    other = move(jnp.where(side_at // HALF == core, here[1], there[1]),
                 lambda s, a, b: owner(s, a, b, True))
    slots = place * row_count + jnp.arange(row_count, dtype=jnp.int32)
    picked = []
    for m in range(micro_count):
        bounds = group_bounds(segment_ids[m])
        holder = jnp.sum((slots[:, None] >= bounds[None, 1:]).astype(jnp.int32), axis=1)
        picked.append(jnp.where((holder == y)[:, None], mine[m], other[m]))
    return jnp.stack(picked)[None]


def solution(mesh):
    return jax.shard_map(
        shards,
        mesh=mesh,
        in_specs=(
            P(None, "dp", None),
            P("section", None),
            P("section", None, "dp"),
            P("section", None, "dp"),
            P("section", None, "dp"),
            P("section", "dp", None),
            P(),
            P(),
            P(),
        ),
        out_specs=P("section", None, "dp", None),
        check_vma=False,
    )
```

```python
import functools

import jax
import jax.numpy as jnp
from jax import lax
from jax.experimental import pallas as pl
from jax.experimental.pallas import tpu as pltpu
from jax.sharding import PartitionSpec as P

DH = 128
SIDE = 4
WINDOW = 128
HALF = WINDOW // 2
STARTS = (0, 32, 96, 128)
AXES = ("section", "dp")


def layer_kernel(turn, place_ref, mine_ref, other_ref, gain_ref, bias_ref, *refs):
    weights, (keep_ref, send_ref) = refs[:8], refs[8:]
    model, width = mine_ref.shape[1], weights[0].shape[1]
    plane, core, start = place_ref[0], place_ref[1], place_ref[2]
    micro = turn - plane

    def weight(j, n, row, rows):
        return weights[2 * j + n // 2][pl.ds((n % 2) * model + row, rows)]

    @pl.when((micro >= 0) & (micro < bias_ref.shape[0]))
    def _():
        wide = jnp.concatenate([mine_ref[...], other_ref[...]], axis=0).astype(jnp.float32)
        mean_square = jnp.mean(wide * wide, axis=-1, keepdims=True)
        normed = (wide * lax.rsqrt(mean_square + 1e-06) * gain_ref[...]).astype(jnp.bfloat16)
        bias = bias_ref[micro]
        context = []
        for j in range(4):
            queries, keyed, values = [
                jnp.dot(
                    normed, weight(j, n, 0, model), preferred_element_type=jnp.float32
                ).astype(jnp.bfloat16)
                for n in range(3)
            ]
            for head in range(width // DH):
                cols = slice(head * DH, (head + 1) * DH)
                scores = lax.dot_general(
                    queries[:, cols], keyed[:, cols], (((1,), (1,)), ((), ())),
                    preferred_element_type=jnp.float32,
                ) * DH ** (-0.5) + bias
                expo = jnp.exp(scores - jnp.max(scores, axis=-1, keepdims=True))
                share = (expo / jnp.sum(expo, axis=-1, keepdims=True)).astype(jnp.bfloat16)
                context.append(
                    jnp.dot(share, values[:, cols], preferred_element_type=jnp.float32)
                    .astype(jnp.bfloat16)
                )
        heads = width // DH
        context = [
            jnp.concatenate(context[j * heads : (j + 1) * heads], axis=1) for j in range(4)
        ]
        row = lax.broadcasted_iota(jnp.int32, (WINDOW, width), 0)
        slot = start + (row + HALF * core) % WINDOW
        live = slot < place_ref[3 + micro]
        for b in range(model // width):
            term = sum(
                jnp.dot(
                    context[j], weight(j, 3, b * width, width), preferred_element_type=jnp.float32
                )
                for j in range(4)
            )
            term = jnp.where(live, term, 0.0).astype(keep_ref.dtype)
            cols = slice(b * width, (b + 1) * width)
            keep_ref[:, cols] = term[:HALF]
            send_ref[:, cols] = term[HALF:]


def run_layer(turn, place, mine, other, gain, biases, weights):
    rows, model = mine.shape
    width = weights[0].shape[1]
    vmem = pl.BlockSpec(memory_space=pltpu.VMEM)
    half = jax.ShapeDtypeStruct((rows, model), jnp.bfloat16)
    resident = [pltpu.with_memory_space_constraint(v, pltpu.VMEM) for v in [biases] + weights]
    return pl.pallas_call(
        functools.partial(layer_kernel, turn),
        out_shape=(half, half),
        in_specs=[pl.BlockSpec(memory_space=pltpu.SMEM)] + [vmem] * 12,
        out_specs=(vmem, vmem),
        compiler_params=pltpu.CompilerParams(vmem_limit_bytes=16 * 1024 * 1024),
        cost_estimate=pl.CostEstimate(
            flops=2 * WINDOW * model * width * 16, bytes_accessed=16 * model * width * 2,
            transcendentals=WINDOW * WINDOW * 8,
        ),
    )(place, mine, other, gain, *resident)


def rms_scale(hidden, norm_gain):
    wide = hidden.astype(jnp.float32)
    mean_square = jnp.mean(wide * wide, axis=-1, keepdims=True)
    return (wide * lax.rsqrt(mean_square + 1e-06) * norm_gain).astype(jnp.bfloat16)


def visible_keys(segments, prefixes, length):
    seq_len = segments.shape[0]
    count_seg = prefixes.shape[0]
    position = jnp.arange(seq_len, dtype=jnp.int32)
    member = segments[:, None] == jnp.arange(count_seg, dtype=jnp.int32)[None, :]
    seg_start = jnp.min(jnp.where(member, position[:, None], jnp.int32(seq_len)), axis=0)
    prefix_end = jnp.sum(jnp.where(member, (seg_start + prefixes)[None, :], jnp.int32(0)), axis=1)
    key_ok = (position[None, :] <= position[:, None]) | (position[None, :] < prefix_end[None, :])
    same_seg = segments[:, None] == segments[None, :]
    live_keys = (position[None, :] < length) | (position[None, :] == position[:, None])
    return same_seg & key_ok & live_keys


def head_terms(hidden, gain, top, bottom, visible):
    seq_len, model = hidden.shape
    width = top.shape[1]
    normed = rms_scale(hidden, gain)
    queries, keyed, values = [
        jnp.dot(normed, w, preferred_element_type=jnp.float32)
        .astype(jnp.bfloat16)
        .reshape(seq_len, width // DH, DH)
        for w in (top[:model], top[model:], bottom[:model])
    ]
    scores = jnp.einsum(
        "qhd,khd->hqk", queries, keyed, preferred_element_type=jnp.float32
    ) * DH ** (-0.5)
    scores = jnp.where(visible[None, :, :], scores, jnp.float32(-1e30))
    expo = jnp.exp(scores - jnp.max(scores, axis=-1, keepdims=True))
    share = (expo / jnp.sum(expo, axis=-1, keepdims=True)).astype(jnp.bfloat16)
    context = jnp.einsum("hqk,khd->qhd", share, values, preferred_element_type=jnp.float32)
    context = context.astype(jnp.bfloat16).reshape(seq_len, width)
    blocks = bottom[model:].reshape(model // width, width, width)
    return jnp.concatenate(
        [
            jnp.dot(context, blocks[b], preferred_element_type=jnp.float32)
            for b in range(model // width)
        ],
        axis=1,
    ).astype(jnp.bfloat16)


def group_bounds(segments):
    seq_len = segments.shape[0]
    quarter = seq_len // SIDE
    position = jnp.arange(seq_len, dtype=jnp.int32)
    before = jnp.concatenate([segments[:1] - 1, segments[:-1]])
    begins = segments != before
    bounds = [jnp.int32(0)]
    for g in range(1, SIDE):
        middle = g * quarter
        low = jnp.max(jnp.where(begins & (position <= middle), position, 0))
        high = jnp.min(jnp.where(begins & (position >= middle), position, seq_len))
        bounds.append(jnp.where(middle - low <= high - middle, low, high))
    return jnp.stack(bounds)


def window_masks(segments, prefixes, length, start, core):
    seq_len = segments.shape[0]
    count_seg = prefixes.shape[0]
    position = jnp.arange(seq_len, dtype=jnp.int32)
    member = segments[:, None] == jnp.arange(count_seg, dtype=jnp.int32)[None, :]
    seg_start = jnp.min(jnp.where(member, position[:, None], jnp.int32(seq_len)), axis=0)
    prefix_end = jnp.sum(jnp.where(member, (seg_start + prefixes)[None, :], jnp.int32(0)), axis=1)

    def halves_of(array):
        return jnp.concatenate([
            lax.dynamic_slice_in_dim(array, start + HALF * core, HALF, 0),
            lax.dynamic_slice_in_dim(array, start + HALF * (1 - core), HALF, 0),
        ])

    seg_w, end_w, pos_w = halves_of(segments), halves_of(prefix_end), halves_of(position)
    key_ok = (pos_w[None, :] <= pos_w[:, None]) | (pos_w[None, :] < end_w[None, :])
    live_keys = (pos_w[None, :] < length) | (pos_w[None, :] == pos_w[:, None])
    visible = (seg_w[:, None] == seg_w[None, :]) & key_ok & live_keys
    return jnp.where(visible, jnp.float32(0.0), jnp.float32(-1e30))


def shards(
    inputs, norm_gain, w_query, w_key, w_value, w_output, segment_ids, prefix_lengths, batch_lengths
):
    section = lax.axis_index("section")
    sections = lax.axis_size("section")
    groups = lax.axis_size("dp")
    place = lax.axis_index("dp")
    micro_count, row_count, model = inputs.shape
    seq_len = row_count * groups
    quarter = seq_len // SIDE
    planes = sections // 2
    plane, core = section // 2, section % 2
    y, x = place // SIDE, place % SIDE
    group, member = (y // 2) * 2 + x // 2, (y % 2) * 2 + x % 2
    start = jnp.asarray(STARTS, jnp.int32)[group]

    def move(value, where):
        pairs = []
        for s in range(sections):
            for a in range(SIDE):
                for b in range(SIDE):
                    to, ta, tb = where(s, a, b)
                    pairs.append((
                        s * groups + a * SIDE + b,
                        (to % sections) * groups + (ta % SIDE) * SIDE + tb % SIDE,
                    ))
        return lax.ppermute(value, AXES, pairs)

    def swap_cores(value):
        return move(value, lambda s, a, b: (s ^ 1, a, b))

    def pack(h):
        width = w_query.shape[2] // 2
        cols = slice(h * width, (h + 1) * width)
        rows = w_output[0, cols]
        blocks = [rows[:, b * width : (b + 1) * width] for b in range(model // width)]
        return (
            jnp.concatenate([w_query[0, :, cols], w_key[0, :, cols]], axis=0),
            jnp.concatenate([w_value[0, :, cols]] + blocks, axis=0),
        )

    first = core == 0
    low, high = pack(0), pack(1)
    kept = [jnp.where(first, p, q) for p, q in zip(low, high)]
    got = [swap_cores(jnp.where(first, q, p)) for p, q in zip(low, high)]
    got_gain = swap_cores(norm_gain)
    gain_a, gain_b = jnp.where(first, norm_gain, got_gain), jnp.where(first, got_gain, norm_gain)

    def over_x(value):
        return move(value, lambda s, a, b: (s, a, b ^ 3))

    def over_y(value):
        return move(value, lambda s, a, b: (s, a ^ 3, b))

    def gather(top, bottom):
        x_top, y_bottom, x_bottom, y_top = over_x(top), over_y(bottom), over_x(bottom), over_y(top)
        far_top, far_bottom = over_y(x_top), over_x(y_bottom)
        return [top, bottom, x_top, x_bottom, y_top, y_bottom, far_top, far_bottom]

    own_a = [jnp.where(first, p, q) for p, q in zip(kept, got)]
    own_b = [jnp.where(first, q, p) for p, q in zip(kept, got)]
    weights_a, weights_b = gather(*own_a), gather(*own_b)

    def ours(pair):
        return jnp.where(first, pair[0], pair[1])

    def gather_rows(rows):
        copies = jnp.broadcast_to(rows[None], (groups, row_count, model))
        return lax.all_to_all(copies, "dp", 0, 0).reshape(seq_len, model)

    def both(value):
        other = swap_cores(value)
        return [jnp.where(first, value, other), jnp.where(first, other, value)]

    visible = [
        visible_keys(segment_ids[m], prefix_lengths[m], batch_lengths[m])
        for m in range(micro_count)
    ]
    slots = place * row_count + jnp.arange(row_count, dtype=jnp.int32)
    live = (slots < ours(batch_lengths))[:, None]

    def spread_layer(rows, full, gain, weights):
        hidden = both(full)
        terms = [
            head_terms(hidden[m], gain, *weights, visible[m]) for m in range(micro_count)
        ]
        chip = (
            ours(terms).astype(jnp.float32) + swap_cores(ours(terms[::-1])).astype(jnp.float32)
        ).astype(jnp.bfloat16)
        pieces = lax.all_to_all(chip.reshape(groups, row_count, model), "dp", 0, 0)
        summed = jnp.sum(pieces.astype(jnp.float32), axis=0)
        return (
            rows.astype(jnp.float32) + jnp.where(live, summed, jnp.float32(0.0))
        ).astype(jnp.bfloat16)

    rows_in = ours(inputs)
    rows_a = spread_layer(rows_in, gather_rows(rows_in), gain_a, own_a)
    rows_b = spread_layer(rows_a, gather_rows(rows_a), gain_b, own_b)
    full = gather_rows(move(rows_b, lambda s, a, b: (s + 2, a, b)))
    stay = lax.dynamic_slice_in_dim(full, start + HALF * core, HALF, 0)
    leave = swap_cores(lax.dynamic_slice_in_dim(full, start + HALF * (1 - core), HALF, 0))
    window_mine = [jnp.where(first, stay, leave), jnp.where(first, leave, stay)]

    biases = jnp.stack([
        window_masks(segment_ids[m], prefix_lengths[m], batch_lengths[m], start, core)
        for m in range(micro_count)
    ])
    where_am_i = jnp.concatenate([
        jnp.stack([plane, core, start]).astype(jnp.int32), batch_lengths.astype(jnp.int32)
    ])

    def one_layer(turn, mine, other, gain, weights):
        keep, send = run_layer(turn, where_am_i, mine, other, gain, biases, weights)
        chip = (
            keep.astype(jnp.float32) + swap_cores(send).astype(jnp.float32)
        ).astype(jnp.bfloat16)
        total = mine.astype(jnp.float32) + chip.astype(jnp.float32)
        for piece in (
            move(chip, lambda s, a, b: (s, a ^ 1, b ^ 1)),
            move(chip, lambda s, a, b: (s, a ^ 1, b)),
            move(chip, lambda s, a, b: (s, a, b ^ 1)),
        ):
            total = total + piece.astype(jnp.float32)
        return total.astype(jnp.bfloat16)

    side = jnp.where(member < SIDE // 2, group + 1, group - 1)
    own_at = (quarter * group + row_count * member - start) % WINDOW
    side_at = (quarter * side + row_count * member - start) % WINDOW

    def blocks(rows):
        return jnp.stack([
            lax.dynamic_slice_in_dim(rows, at % HALF, row_count, 0) for at in (own_at, side_at)
        ])

    blank = jnp.zeros((2, row_count, model), jnp.bfloat16)
    stash = [[blank] * micro_count, [blank] * micro_count]

    def keep_blocks(layer, turn, rows):
        found = blocks(rows)
        for m in range(micro_count):
            if 1 <= turn - m < planes:
                stash[layer][m] = jnp.where(plane == turn - m, found, stash[layer][m])

    mine = window_mine[0]
    turns = planes + micro_count - 1
    for turn in range(1, turns):
        out_a = one_layer(turn, mine, swap_cores(mine), gain_a, weights_a)
        out_b = one_layer(turn, out_a, swap_cores(out_a), gain_b, weights_b)
        if turn < turns - 1:
            mine = move(out_b, lambda s, a, b: (s + 2, a, b))
            if turn < micro_count:
                mine = jnp.where(plane == 1, window_mine[turn], mine)
        keep_blocks(0, turn, out_a)
        keep_blocks(1, turn, out_b)

    stash_a, stash_b = [jnp.stack(rows, axis=1) for rows in stash]
    here = jnp.where(first, stash_a, stash_b)
    there = swap_cores(jnp.where(first, stash_b, stash_a))

    def owner(s, a, b, shift):
        g, t = (a // 2) * 2 + b // 2, (a % 2) * 2 + b % 2
        return (s, g + (0 if not shift else 1 if t < SIDE // 2 else -1), t)

    mine = move(jnp.where(own_at // HALF == core, here[0], there[0]),
                lambda s, a, b: owner(s, a, b, False))
    other = move(jnp.where(side_at // HALF == core, here[1], there[1]),
                 lambda s, a, b: owner(s, a, b, True))
    kept_rows, got_rows = ours([rows_a, rows_b]), swap_cores(ours([rows_b, rows_a]))
    early = [jnp.where(first, kept_rows, got_rows), jnp.where(first, got_rows, kept_rows)]
    picked = []
    for m in range(micro_count):
        bounds = group_bounds(segment_ids[m])
        holder = jnp.sum((slots[:, None] >= bounds[None, 1:]).astype(jnp.int32), axis=1)
        late = jnp.where((holder == y)[:, None], mine[m], other[m])
        picked.append(jnp.where(plane == 0, early[m], late))
    return jnp.stack(picked)[None]


def solution(mesh):
    return jax.shard_map(
        shards,
        mesh=mesh,
        in_specs=(
            P(None, "dp", None),
            P("section", None),
            P("section", None, "dp"),
            P("section", None, "dp"),
            P("section", None, "dp"),
            P("section", "dp", None),
            P(),
            P(),
            P(),
        ),
        out_specs=P("section", None, "dp", None),
        check_vma=False,
    )
```

```python
import functools

import jax
import jax.numpy as jnp
from jax import lax
from jax.experimental import pallas as pl
from jax.experimental.pallas import tpu as pltpu
from jax.sharding import PartitionSpec as P

DH = 128
SIDE = 4
WINDOW = 128
HALF = WINDOW // 2
STARTS = (0, 32, 96, 128)
AXES = ("section", "dp")


def layer_kernel(turn, place_ref, mine_ref, other_ref, gain_ref, bias_ref, *refs):
    weights, (keep_ref, send_ref) = refs[:8], refs[8:]
    model, width = mine_ref.shape[1], weights[0].shape[1]
    plane, core, start = place_ref[0], place_ref[1], place_ref[2]
    micro = turn - plane

    def weight(j, n, row, rows):
        return weights[2 * j + n // 2][pl.ds((n % 2) * model + row, rows)]

    @pl.when((micro >= 0) & (micro < bias_ref.shape[0]))
    def _():
        wide = jnp.concatenate([mine_ref[...], other_ref[...]], axis=0).astype(jnp.float32)
        mean_square = jnp.mean(wide * wide, axis=-1, keepdims=True)
        normed = (wide * lax.rsqrt(mean_square + 1e-06) * gain_ref[...]).astype(jnp.bfloat16)
        bias = bias_ref[micro]
        context = []
        for j in range(4):
            queries, keyed, values = [
                jnp.dot(
                    normed, weight(j, n, 0, model), preferred_element_type=jnp.float32
                ).astype(jnp.bfloat16)
                for n in range(3)
            ]
            for head in range(width // DH):
                cols = slice(head * DH, (head + 1) * DH)
                scores = lax.dot_general(
                    queries[:, cols], keyed[:, cols], (((1,), (1,)), ((), ())),
                    preferred_element_type=jnp.float32,
                ) * DH ** (-0.5) + bias
                expo = jnp.exp(scores - jnp.max(scores, axis=-1, keepdims=True))
                share = (expo / jnp.sum(expo, axis=-1, keepdims=True)).astype(jnp.bfloat16)
                context.append(
                    jnp.dot(share, values[:, cols], preferred_element_type=jnp.float32)
                    .astype(jnp.bfloat16)
                )
        heads = width // DH
        context = [
            jnp.concatenate(context[j * heads : (j + 1) * heads], axis=1) for j in range(4)
        ]
        row = lax.broadcasted_iota(jnp.int32, (WINDOW, width), 0)
        slot = start + (row + HALF * core) % WINDOW
        live = slot < place_ref[3 + micro]
        for b in range(model // width):
            term = sum(
                jnp.dot(
                    context[j], weight(j, 3, b * width, width), preferred_element_type=jnp.float32
                )
                for j in range(4)
            )
            term = jnp.where(live, term, 0.0).astype(keep_ref.dtype)
            cols = slice(b * width, (b + 1) * width)
            keep_ref[:, cols] = term[:HALF]
            send_ref[:, cols] = term[HALF:]


def settle_kernel(top_ref, bottom_ref, top_out, bottom_out, sems):
    copies = [
        pltpu.make_async_copy(top_ref, top_out, sems.at[0]),
        pltpu.make_async_copy(bottom_ref, bottom_out, sems.at[1]),
    ]
    for copy in copies:
        copy.start()
    for copy in copies:
        copy.wait()


def settle(pair):
    return list(pl.pallas_call(
        settle_kernel,
        out_shape=tuple(pltpu.VMEM(v.shape, v.dtype) for v in pair),
        in_specs=[pl.BlockSpec(memory_space=pl.ANY)] * 2,
        out_specs=(pl.BlockSpec(memory_space=pltpu.VMEM),) * 2,
        scratch_shapes=[pltpu.SemaphoreType.DMA((2,))],
        compiler_params=pltpu.CompilerParams(vmem_limit_bytes=8 * 1024 * 1024),
    )(*pair))


def run_layer(turn, place, mine, other, gain, biases, weights):
    rows, model = mine.shape
    width = weights[0].shape[1]
    vmem = pl.BlockSpec(memory_space=pltpu.VMEM)
    half = jax.ShapeDtypeStruct((rows, model), jnp.bfloat16)
    resident = [pltpu.with_memory_space_constraint(v, pltpu.VMEM) for v in [biases] + weights]
    return pl.pallas_call(
        functools.partial(layer_kernel, turn),
        out_shape=(half, half),
        in_specs=[pl.BlockSpec(memory_space=pltpu.SMEM)] + [vmem] * 12,
        out_specs=(vmem, vmem),
        compiler_params=pltpu.CompilerParams(vmem_limit_bytes=16 * 1024 * 1024),
        cost_estimate=pl.CostEstimate(
            flops=2 * WINDOW * model * width * 16, bytes_accessed=16 * model * width * 2,
            transcendentals=WINDOW * WINDOW * 8,
        ),
    )(place, mine, other, gain, *resident)


def group_bounds(segments):
    seq_len = segments.shape[0]
    quarter = seq_len // SIDE
    position = jnp.arange(seq_len, dtype=jnp.int32)
    before = jnp.concatenate([segments[:1] - 1, segments[:-1]])
    begins = segments != before
    bounds = [jnp.int32(0)]
    for g in range(1, SIDE):
        middle = g * quarter
        low = jnp.max(jnp.where(begins & (position <= middle), position, 0))
        high = jnp.min(jnp.where(begins & (position >= middle), position, seq_len))
        bounds.append(jnp.where(middle - low <= high - middle, low, high))
    return jnp.stack(bounds)


def window_masks(segments, prefixes, length, start, core):
    seq_len = segments.shape[0]
    count_seg = prefixes.shape[0]
    position = jnp.arange(seq_len, dtype=jnp.int32)
    member = segments[:, None] == jnp.arange(count_seg, dtype=jnp.int32)[None, :]
    seg_start = jnp.min(jnp.where(member, position[:, None], jnp.int32(seq_len)), axis=0)
    prefix_end = jnp.sum(jnp.where(member, (seg_start + prefixes)[None, :], jnp.int32(0)), axis=1)

    def halves_of(array):
        return jnp.concatenate([
            lax.dynamic_slice_in_dim(array, start + HALF * core, HALF, 0),
            lax.dynamic_slice_in_dim(array, start + HALF * (1 - core), HALF, 0),
        ])

    seg_w, end_w, pos_w = halves_of(segments), halves_of(prefix_end), halves_of(position)
    key_ok = (pos_w[None, :] <= pos_w[:, None]) | (pos_w[None, :] < end_w[None, :])
    live_keys = (pos_w[None, :] < length) | (pos_w[None, :] == pos_w[:, None])
    visible = (seg_w[:, None] == seg_w[None, :]) & key_ok & live_keys
    return jnp.where(visible, jnp.float32(0.0), jnp.float32(-1e30))


def shards(
    inputs, norm_gain, w_query, w_key, w_value, w_output, segment_ids, prefix_lengths, batch_lengths
):
    section = lax.axis_index("section")
    sections = lax.axis_size("section")
    groups = lax.axis_size("dp")
    place = lax.axis_index("dp")
    micro_count, row_count, model = inputs.shape
    seq_len = row_count * groups
    quarter = seq_len // SIDE
    planes = sections // 2
    plane, core = section // 2, section % 2
    y, x = place // SIDE, place % SIDE
    group, member = (y // 2) * 2 + x // 2, (y % 2) * 2 + x % 2
    start = jnp.asarray(STARTS, jnp.int32)[group]

    def move(value, where):
        pairs = []
        for s in range(sections):
            for a in range(SIDE):
                for b in range(SIDE):
                    to, ta, tb = where(s, a, b)
                    pairs.append((
                        s * groups + a * SIDE + b,
                        (to % sections) * groups + (ta % SIDE) * SIDE + tb % SIDE,
                    ))
        return lax.ppermute(value, AXES, pairs)

    def swap_cores(value):
        return move(value, lambda s, a, b: (s ^ 1, a, b))

    def pack(h):
        width = w_query.shape[2] // 2
        cols = slice(h * width, (h + 1) * width)
        rows = w_output[0, cols]
        blocks = [rows[:, b * width : (b + 1) * width] for b in range(model // width)]
        return (
            jnp.concatenate([w_query[0, :, cols], w_key[0, :, cols]], axis=0),
            jnp.concatenate([w_value[0, :, cols]] + blocks, axis=0),
        )

    first = core == 0
    low, high = pack(0), pack(1)
    kept = [jnp.where(first, p, q) for p, q in zip(low, high)]
    got = [swap_cores(jnp.where(first, q, p)) for p, q in zip(low, high)]
    got_gain = swap_cores(norm_gain)
    gain_a, gain_b = jnp.where(first, norm_gain, got_gain), jnp.where(first, got_gain, norm_gain)

    def over_x(value):
        return move(value, lambda s, a, b: (s, a, b ^ 3))

    def over_y(value):
        return move(value, lambda s, a, b: (s, a ^ 3, b))

    def near(top, bottom):
        return [over_x(top), over_y(bottom), over_x(bottom), over_y(top)]

    def shards_of(own, x_top, y_bottom, x_bottom, y_top):
        far = [over_y(x_top), over_x(y_bottom)]
        return settle(own) + [x_top, x_bottom, y_top, y_bottom] + far

    own_a = [jnp.where(first, p, q) for p, q in zip(kept, got)]
    own_b = [jnp.where(first, q, p) for p, q in zip(kept, got)]
    near_a = near(*own_a)
    own_b, near_a[:2] = lax.optimization_barrier((own_b, near_a[:2]))
    weights_a = shards_of(own_a, *near_a)
    weights_b = shards_of(own_b, *near(*own_b))

    inputs_all = lax.all_gather(inputs, "dp", axis=1, tiled=True)
    window_mine = lax.dynamic_slice_in_dim(inputs_all, start + HALF * core, HALF, 1)
    window_other = lax.dynamic_slice_in_dim(inputs_all, start + HALF * (1 - core), HALF, 1)

    biases = jnp.stack([
        window_masks(segment_ids[m], prefix_lengths[m], batch_lengths[m], start, core)
        for m in range(micro_count)
    ])
    where_am_i = jnp.concatenate([
        jnp.stack([plane, core, start]).astype(jnp.int32), batch_lengths.astype(jnp.int32)
    ])

    def one_layer(turn, mine, other, gain, weights):
        keep, send = run_layer(turn, where_am_i, mine, other, gain, biases, weights)
        chip = (
            keep.astype(jnp.float32) + swap_cores(send).astype(jnp.float32)
        ).astype(jnp.bfloat16)
        total = mine.astype(jnp.float32) + chip.astype(jnp.float32)
        for piece in (
            move(chip, lambda s, a, b: (s, a ^ 1, b ^ 1)),
            move(chip, lambda s, a, b: (s, a ^ 1, b)),
            move(chip, lambda s, a, b: (s, a, b ^ 1)),
        ):
            total = total + piece.astype(jnp.float32)
        return total.astype(jnp.bfloat16)

    own_at = quarter * group + row_count * member - start
    side = jnp.where(member < SIDE // 2, group + 1, group - 1)
    side_at = (quarter * side + row_count * member - start) % WINDOW
    at = jnp.where(own_at // HALF == core, own_at, side_at) % HALF
    blank = jnp.zeros((row_count, model), jnp.bfloat16)
    stash = [[blank] * micro_count, [blank] * micro_count]

    def keep_block(layer, turn, rows):
        found = lax.dynamic_slice_in_dim(rows, at, row_count, 0)
        for m in range(micro_count):
            if 0 <= turn - m < planes:
                stash[layer][m] = jnp.where(plane == turn - m, found, stash[layer][m])

    mine, other = window_mine[0], window_other[0]
    turns = planes + micro_count - 1
    for turn in range(turns):
        out_a = one_layer(turn, mine, other, gain_a, weights_a)
        out_b = one_layer(turn, out_a, swap_cores(out_a), gain_b, weights_b)
        if turn < turns - 1:
            onward = (
                jnp.where(plane == planes - 1, window_mine[1], out_b) if turn == 0 else out_b
            )
            mine = move(onward, lambda s, a, b: (s + 2, a, b))
            other = swap_cores(mine)
        keep_block(0, turn, out_a)
        keep_block(1, turn, out_b)

    def owner(s, a, b):
        g, t = (a // 2) * 2 + b // 2, (a % 2) * 2 + b % 2
        lower = t < SIDE // 2
        own_half = (quarter * g + row_count * t - STARTS[g]) // HALF
        to_core, to = (0 if lower else 1), g
        if s % 2 != own_half:
            to_core, to = 1 - to_core, (g + (1 if lower else -1)) % SIDE
        return (s - s % 2 + to_core, to, t)

    moved = move(jnp.stack([jnp.stack(rows) for rows in stash]), owner)
    stash_a, stash_b = moved[0], moved[1]
    here = jnp.where(first, stash_a, stash_b)
    there = swap_cores(jnp.where(first, stash_b, stash_a))
    has_own = first == (x < SIDE // 2)
    mine, other = jnp.where(has_own, here, there), jnp.where(has_own, there, here)
    slots = place * row_count + jnp.arange(row_count, dtype=jnp.int32)
    picked = []
    for m in range(micro_count):
        bounds = group_bounds(segment_ids[m])
        holder = jnp.sum((slots[:, None] >= bounds[None, 1:]).astype(jnp.int32), axis=1)
        picked.append(jnp.where((holder == y)[:, None], mine[m], other[m]))
    return jnp.stack(picked)[None]


def solution(mesh):
    return jax.shard_map(
        shards,
        mesh=mesh,
        in_specs=(
            P(None, "dp", None),
            P("section", None),
            P("section", None, "dp"),
            P("section", None, "dp"),
            P("section", None, "dp"),
            P("section", "dp", None),
            P(),
            P(),
            P(),
        ),
        out_specs=P("section", None, "dp", None),
        check_vma=False,
    )
```

```python
import functools

import jax
import jax.numpy as jnp
from jax import lax
from jax.experimental import pallas as pl
from jax.experimental.pallas import tpu as pltpu
from jax.sharding import PartitionSpec as P

DH = 128
SIDE = 4
WINDOW = 128
HALF = WINDOW // 2
STARTS = (0, 32, 96, 128)
AXES = ("section", "dp")


def layer_kernel(turn, place_ref, mine_ref, other_ref, gain_ref, bias_ref, *refs):
    weights, (keep_ref, send_ref) = refs[:8], refs[8:]
    model, width = mine_ref.shape[1], weights[0].shape[1]
    plane, core, start = place_ref[0], place_ref[1], place_ref[2]
    micro = turn - plane

    def weight(j, n, row, rows):
        return weights[2 * j + n // 2][pl.ds((n % 2) * model + row, rows)]

    @pl.when((micro >= 0) & (micro < bias_ref.shape[0]))
    def _():
        wide = jnp.concatenate([mine_ref[...], other_ref[...]], axis=0).astype(jnp.float32)
        mean_square = jnp.mean(wide * wide, axis=-1, keepdims=True)
        normed = (wide * lax.rsqrt(mean_square + 1e-06) * gain_ref[...]).astype(jnp.bfloat16)
        bias = bias_ref[micro]
        context = []
        for j in range(4):
            queries, keyed, values = [
                jnp.dot(
                    normed, weight(j, n, 0, model), preferred_element_type=jnp.float32
                ).astype(jnp.bfloat16)
                for n in range(3)
            ]
            for head in range(width // DH):
                cols = slice(head * DH, (head + 1) * DH)
                scores = lax.dot_general(
                    queries[:, cols], keyed[:, cols], (((1,), (1,)), ((), ())),
                    preferred_element_type=jnp.float32,
                ) * DH ** (-0.5) + bias
                expo = jnp.exp(scores - jnp.max(scores, axis=-1, keepdims=True))
                share = (expo / jnp.sum(expo, axis=-1, keepdims=True)).astype(jnp.bfloat16)
                context.append(
                    jnp.dot(share, values[:, cols], preferred_element_type=jnp.float32)
                    .astype(jnp.bfloat16)
                )
        heads = width // DH
        context = [
            jnp.concatenate(context[j * heads : (j + 1) * heads], axis=1) for j in range(4)
        ]
        row = lax.broadcasted_iota(jnp.int32, (WINDOW, width), 0)
        slot = start + (row + HALF * core) % WINDOW
        live = slot < place_ref[3 + micro]
        for b in range(model // width):
            term = sum(
                jnp.dot(
                    context[j], weight(j, 3, b * width, width), preferred_element_type=jnp.float32
                )
                for j in range(4)
            )
            term = jnp.where(live, term, 0.0).astype(keep_ref.dtype)
            cols = slice(b * width, (b + 1) * width)
            keep_ref[:, cols] = term[:HALF]
            send_ref[:, cols] = term[HALF:]


def settle_kernel(top_ref, bottom_ref, top_out, bottom_out, sems):
    copies = [
        pltpu.make_async_copy(top_ref, top_out, sems.at[0]),
        pltpu.make_async_copy(bottom_ref, bottom_out, sems.at[1]),
    ]
    for copy in copies:
        copy.start()
    for copy in copies:
        copy.wait()


def settle(pair):
    return list(pl.pallas_call(
        settle_kernel,
        out_shape=tuple(pltpu.VMEM(v.shape, v.dtype) for v in pair),
        in_specs=[pl.BlockSpec(memory_space=pl.ANY)] * 2,
        out_specs=(pl.BlockSpec(memory_space=pltpu.VMEM),) * 2,
        scratch_shapes=[pltpu.SemaphoreType.DMA((2,))],
        compiler_params=pltpu.CompilerParams(vmem_limit_bytes=6 * 1024 * 1024),
    )(*pair))


def run_layer(turn, place, mine, other, gain, biases, weights):
    rows, model = mine.shape
    width = weights[0].shape[1]
    vmem = pl.BlockSpec(memory_space=pltpu.VMEM)
    half = jax.ShapeDtypeStruct((rows, model), jnp.bfloat16)
    resident = [pltpu.with_memory_space_constraint(v, pltpu.VMEM) for v in [biases] + weights]
    return pl.pallas_call(
        functools.partial(layer_kernel, turn),
        out_shape=(half, half),
        in_specs=[pl.BlockSpec(memory_space=pltpu.SMEM)] + [vmem] * 12,
        out_specs=(vmem, vmem),
        compiler_params=pltpu.CompilerParams(vmem_limit_bytes=6 * 1024 * 1024),
        cost_estimate=pl.CostEstimate(
            flops=2 * WINDOW * model * width * 16, bytes_accessed=16 * model * width * 2,
            transcendentals=WINDOW * WINDOW * 8,
        ),
    )(place, mine, other, gain, *resident)


def group_bounds(segments):
    seq_len = segments.shape[0]
    quarter = seq_len // SIDE
    position = jnp.arange(seq_len, dtype=jnp.int32)
    before = jnp.concatenate([segments[:1] - 1, segments[:-1]])
    begins = segments != before
    bounds = [jnp.int32(0)]
    for g in range(1, SIDE):
        middle = g * quarter
        low = jnp.max(jnp.where(begins & (position <= middle), position, 0))
        high = jnp.min(jnp.where(begins & (position >= middle), position, seq_len))
        bounds.append(jnp.where(middle - low <= high - middle, low, high))
    return jnp.stack(bounds)


def window_masks(segments, prefixes, length, start, core):
    seq_len = segments.shape[0]
    count_seg = prefixes.shape[0]
    position = jnp.arange(seq_len, dtype=jnp.int32)
    member = segments[:, None] == jnp.arange(count_seg, dtype=jnp.int32)[None, :]
    seg_start = jnp.min(jnp.where(member, position[:, None], jnp.int32(seq_len)), axis=0)
    prefix_end = jnp.sum(jnp.where(member, (seg_start + prefixes)[None, :], jnp.int32(0)), axis=1)

    def halves_of(array):
        return jnp.concatenate([
            lax.dynamic_slice_in_dim(array, start + HALF * core, HALF, 0),
            lax.dynamic_slice_in_dim(array, start + HALF * (1 - core), HALF, 0),
        ])

    seg_w, end_w, pos_w = halves_of(segments), halves_of(prefix_end), halves_of(position)
    key_ok = (pos_w[None, :] <= pos_w[:, None]) | (pos_w[None, :] < end_w[None, :])
    live_keys = (pos_w[None, :] < length) | (pos_w[None, :] == pos_w[:, None])
    visible = (seg_w[:, None] == seg_w[None, :]) & key_ok & live_keys
    return jnp.where(visible, jnp.float32(0.0), jnp.float32(-1e30))


def shards(
    inputs, norm_gain, w_query, w_key, w_value, w_output, segment_ids, prefix_lengths, batch_lengths
):
    section = lax.axis_index("section")
    sections = lax.axis_size("section")
    groups = lax.axis_size("dp")
    place = lax.axis_index("dp")
    micro_count, row_count, model = inputs.shape
    seq_len = row_count * groups
    quarter = seq_len // SIDE
    planes = sections // 2
    plane, core = section // 2, section % 2
    y, x = place // SIDE, place % SIDE
    group, member = (y // 2) * 2 + x // 2, (y % 2) * 2 + x % 2
    start = jnp.asarray(STARTS, jnp.int32)[group]

    def move(value, where):
        pairs = []
        for s in range(sections):
            for a in range(SIDE):
                for b in range(SIDE):
                    to, ta, tb = where(s, a, b)
                    pairs.append((
                        s * groups + a * SIDE + b,
                        (to % sections) * groups + (ta % SIDE) * SIDE + tb % SIDE,
                    ))
        return lax.ppermute(value, AXES, pairs)

    def swap_cores(value):
        return move(value, lambda s, a, b: (s ^ 1, a, b))

    def pack(h):
        width = w_query.shape[2] // 2
        cols = slice(h * width, (h + 1) * width)
        rows = w_output[0, cols]
        blocks = [rows[:, b * width : (b + 1) * width] for b in range(model // width)]
        return (
            jnp.concatenate([w_query[0, :, cols], w_key[0, :, cols]], axis=0),
            jnp.concatenate([w_value[0, :, cols]] + blocks, axis=0),
        )

    first = core == 0
    low, high = pack(0), pack(1)
    kept = [jnp.where(first, p, q) for p, q in zip(low, high)]
    got = [swap_cores(jnp.where(first, q, p)) for p, q in zip(low, high)]
    got_gain = swap_cores(norm_gain)
    gain_a, gain_b = jnp.where(first, norm_gain, got_gain), jnp.where(first, got_gain, norm_gain)

    def over_x(value):
        return move(value, lambda s, a, b: (s, a, b ^ 3))

    def over_y(value):
        return move(value, lambda s, a, b: (s, a ^ 3, b))

    def near(top, bottom):
        return [over_x(top), over_y(bottom), over_x(bottom), over_y(top)]

    def shards_of(own, x_top, y_bottom, x_bottom, y_top):
        far = [over_y(x_top), over_x(y_bottom)]
        return settle(own) + [x_top, x_bottom, y_top, y_bottom] + far

    own_a = [jnp.where(first, p, q) for p, q in zip(kept, got)]
    own_b = [jnp.where(first, q, p) for p, q in zip(kept, got)]
    near_a = near(*own_a)
    own_b, near_a[:2] = lax.optimization_barrier((own_b, near_a[:2]))
    weights_a = shards_of(own_a, *near_a)
    weights_b = shards_of(own_b, *near(*own_b))

    inputs_all = lax.all_gather(inputs, "dp", axis=1, tiled=True)
    window_mine = lax.dynamic_slice_in_dim(inputs_all, start + HALF * core, HALF, 1)
    window_other = lax.dynamic_slice_in_dim(inputs_all, start + HALF * (1 - core), HALF, 1)

    slots = place * row_count + jnp.arange(row_count, dtype=jnp.int32)
    holders = [
        jnp.sum(
            (slots[:, None] >= group_bounds(segment_ids[m])[None, 1:]).astype(jnp.int32), axis=1
        )
        for m in range(micro_count)
    ]
    window_mine, holders = lax.optimization_barrier((window_mine, holders))

    biases = jnp.stack([
        window_masks(segment_ids[m], prefix_lengths[m], batch_lengths[m], start, core)
        for m in range(micro_count)
    ])
    where_am_i = jnp.concatenate([
        jnp.stack([plane, core, start]).astype(jnp.int32), batch_lengths.astype(jnp.int32)
    ])

    def one_layer(turn, mine, other, gain, weights):
        keep, send = run_layer(turn, where_am_i, mine, other, gain, biases, weights)
        chip = (
            keep.astype(jnp.float32) + swap_cores(send).astype(jnp.float32)
        ).astype(jnp.bfloat16)
        total = mine.astype(jnp.float32) + chip.astype(jnp.float32)
        for piece in (
            move(chip, lambda s, a, b: (s, a ^ 1, b ^ 1)),
            move(chip, lambda s, a, b: (s, a ^ 1, b)),
            move(chip, lambda s, a, b: (s, a, b ^ 1)),
        ):
            total = total + piece.astype(jnp.float32)
        return total.astype(jnp.bfloat16)

    own_at = quarter * group + row_count * member - start
    side = jnp.where(member < SIDE // 2, group + 1, group - 1)
    side_at = (quarter * side + row_count * member - start) % WINDOW
    at = jnp.where(own_at // HALF == core, own_at, side_at) % HALF
    blank = jnp.zeros((row_count, model), jnp.bfloat16)
    stash = [[blank] * micro_count, [blank] * micro_count]

    def keep_block(layer, turn, rows):
        found = lax.dynamic_slice_in_dim(rows, at, row_count, 0)
        for m in range(micro_count):
            if 0 <= turn - m < planes:
                stash[layer][m] = jnp.where(plane == turn - m, found, stash[layer][m])

    mine, other = window_mine[0], window_other[0]
    turns = planes + micro_count - 1
    for turn in range(turns):
        out_a = one_layer(turn, mine, other, gain_a, weights_a)
        out_b = one_layer(turn, out_a, swap_cores(out_a), gain_b, weights_b)
        if turn < turns - 1:
            onward = (
                jnp.where(plane == planes - 1, window_mine[1], out_b) if turn == 0 else out_b
            )
            mine = move(onward, lambda s, a, b: (s + 2, a, b))
            other = swap_cores(mine)
        keep_block(0, turn, out_a)
        keep_block(1, turn, out_b)

    def owner(s, a, b):
        g, t = (a // 2) * 2 + b // 2, (a % 2) * 2 + b % 2
        lower = t < SIDE // 2
        own_half = (quarter * g + row_count * t - STARTS[g]) // HALF
        to_core, to = (0 if lower else 1), g
        if s % 2 != own_half:
            to_core, to = 1 - to_core, (g + (1 if lower else -1)) % SIDE
        return (s - s % 2 + to_core, to, t)

    moved = move(jnp.stack([jnp.stack(rows) for rows in stash]), owner)
    stash_a, stash_b = moved[0], moved[1]
    here = jnp.where(first, stash_a, stash_b)
    there = swap_cores(jnp.where(first, stash_b, stash_a))
    has_own = first == (x < SIDE // 2)
    mine, other = jnp.where(has_own, here, there), jnp.where(has_own, there, here)
    picked = [
        jnp.where((holders[m] == y)[:, None], mine[m], other[m]) for m in range(micro_count)
    ]
    return jnp.stack(picked)[None]


def solution(mesh):
    return jax.shard_map(
        shards,
        mesh=mesh,
        in_specs=(
            P(None, "dp", None),
            P("section", None),
            P("section", None, "dp"),
            P("section", None, "dp"),
            P("section", None, "dp"),
            P("section", "dp", None),
            P(),
            P(),
            P(),
        ),
        out_specs=P("section", None, "dp", None),
        check_vma=False,
    )
```

```python
import functools

import jax
import jax.numpy as jnp
from jax import lax
from jax.experimental import pallas as pl
from jax.experimental.pallas import tpu as pltpu
from jax.sharding import PartitionSpec as P

DH = 128
SIDE = 4
WINDOW = 128
HALF = WINDOW // 2
STARTS = (0, 32, 96, 128)
AXES = ("section", "dp")


def layer_kernel(turn, place_ref, mine_ref, other_ref, gain_ref, bias_ref, *refs):
    weights, (keep_ref, send_ref) = refs[:8], refs[8:]
    model, width = mine_ref.shape[1], weights[0].shape[1]
    plane, core, start = place_ref[0], place_ref[1], place_ref[2]
    micro = turn - plane

    def weight(j, n, row, rows):
        return weights[2 * j + n // 2][pl.ds((n % 2) * model + row, rows)]

    @pl.when((micro >= 0) & (micro < bias_ref.shape[0]))
    def _():
        wide = jnp.concatenate([mine_ref[...], other_ref[...]], axis=0).astype(jnp.float32)
        mean_square = jnp.mean(wide * wide, axis=-1, keepdims=True)
        normed = (wide * lax.rsqrt(mean_square + 1e-06) * gain_ref[...]).astype(jnp.bfloat16)
        bias = bias_ref[micro]
        context = []
        for j in range(4):
            queries, keyed, values = [
                jnp.dot(
                    normed, weight(j, n, 0, model), preferred_element_type=jnp.float32
                ).astype(jnp.bfloat16)
                for n in range(3)
            ]
            for head in range(width // DH):
                cols = slice(head * DH, (head + 1) * DH)
                scores = lax.dot_general(
                    queries[:, cols], keyed[:, cols], (((1,), (1,)), ((), ())),
                    preferred_element_type=jnp.float32,
                ) * DH ** (-0.5) + bias
                expo = jnp.exp(scores - jnp.max(scores, axis=-1, keepdims=True))
                share = (expo / jnp.sum(expo, axis=-1, keepdims=True)).astype(jnp.bfloat16)
                context.append(
                    jnp.dot(share, values[:, cols], preferred_element_type=jnp.float32)
                    .astype(jnp.bfloat16)
                )
        heads = width // DH
        context = [
            jnp.concatenate(context[j * heads : (j + 1) * heads], axis=1) for j in range(4)
        ]
        row = lax.broadcasted_iota(jnp.int32, (WINDOW, width), 0)
        slot = start + (row + HALF * core) % WINDOW
        live = slot < place_ref[3 + micro]
        for b in range(model // width):
            term = sum(
                jnp.dot(
                    context[j], weight(j, 3, b * width, width), preferred_element_type=jnp.float32
                )
                for j in range(4)
            )
            term = jnp.where(live, term, 0.0).astype(keep_ref.dtype)
            cols = slice(b * width, (b + 1) * width)
            keep_ref[:, cols] = term[:HALF]
            send_ref[:, cols] = term[HALF:]


def settle_kernel(top_ref, bottom_ref, top_out, bottom_out, sems):
    copies = [
        pltpu.make_async_copy(top_ref, top_out, sems.at[0]),
        pltpu.make_async_copy(bottom_ref, bottom_out, sems.at[1]),
    ]
    for copy in copies:
        copy.start()
    for copy in copies:
        copy.wait()


def settle(pair):
    return list(pl.pallas_call(
        settle_kernel,
        out_shape=tuple(pltpu.VMEM(v.shape, v.dtype) for v in pair),
        in_specs=[pl.BlockSpec(memory_space=pl.ANY)] * 2,
        out_specs=(pl.BlockSpec(memory_space=pltpu.VMEM),) * 2,
        scratch_shapes=[pltpu.SemaphoreType.DMA((2,))],
        compiler_params=pltpu.CompilerParams(vmem_limit_bytes=6 * 1024 * 1024),
    )(*pair))


def run_layer(turn, place, mine, other, gain, biases, weights):
    rows, model = mine.shape
    width = weights[0].shape[1]
    vmem = pl.BlockSpec(memory_space=pltpu.VMEM)
    half = jax.ShapeDtypeStruct((rows, model), jnp.bfloat16)
    resident = [pltpu.with_memory_space_constraint(v, pltpu.VMEM) for v in [biases] + weights]
    return pl.pallas_call(
        functools.partial(layer_kernel, turn),
        out_shape=(half, half),
        in_specs=[pl.BlockSpec(memory_space=pltpu.SMEM)] + [vmem] * 12,
        out_specs=(vmem, vmem),
        compiler_params=pltpu.CompilerParams(vmem_limit_bytes=6 * 1024 * 1024),
        cost_estimate=pl.CostEstimate(
            flops=2 * WINDOW * model * width * 16, bytes_accessed=16 * model * width * 2,
            transcendentals=WINDOW * WINDOW * 8,
        ),
    )(place, mine, other, gain, *resident)


def group_bounds(segments):
    seq_len = segments.shape[0]
    quarter = seq_len // SIDE
    position = jnp.arange(seq_len, dtype=jnp.int32)
    before = jnp.concatenate([segments[:1] - 1, segments[:-1]])
    begins = segments != before
    bounds = [jnp.int32(0)]
    for g in range(1, SIDE):
        middle = g * quarter
        low = jnp.max(jnp.where(begins & (position <= middle), position, 0))
        high = jnp.min(jnp.where(begins & (position >= middle), position, seq_len))
        bounds.append(jnp.where(middle - low <= high - middle, low, high))
    return jnp.stack(bounds)


def window_masks(segments, prefixes, length, start, core):
    seq_len = segments.shape[0]
    count_seg = prefixes.shape[0]
    position = jnp.arange(seq_len, dtype=jnp.int32)
    member = segments[:, None] == jnp.arange(count_seg, dtype=jnp.int32)[None, :]
    seg_start = jnp.min(jnp.where(member, position[:, None], jnp.int32(seq_len)), axis=0)
    prefix_end = jnp.sum(jnp.where(member, (seg_start + prefixes)[None, :], jnp.int32(0)), axis=1)

    def halves_of(array):
        return jnp.concatenate([
            lax.dynamic_slice_in_dim(array, start + HALF * core, HALF, 0),
            lax.dynamic_slice_in_dim(array, start + HALF * (1 - core), HALF, 0),
        ])

    seg_w, end_w, pos_w = halves_of(segments), halves_of(prefix_end), halves_of(position)
    key_ok = (pos_w[None, :] <= pos_w[:, None]) | (pos_w[None, :] < end_w[None, :])
    live_keys = (pos_w[None, :] < length) | (pos_w[None, :] == pos_w[:, None])
    visible = (seg_w[:, None] == seg_w[None, :]) & key_ok & live_keys
    return jnp.where(visible, jnp.float32(0.0), jnp.float32(-1e30))


def shards(
    inputs, norm_gain, w_query, w_key, w_value, w_output, segment_ids, prefix_lengths, batch_lengths
):
    section = lax.axis_index("section")
    sections = lax.axis_size("section")
    groups = lax.axis_size("dp")
    place = lax.axis_index("dp")
    micro_count, row_count, model = inputs.shape
    seq_len = row_count * groups
    quarter = seq_len // SIDE
    planes = sections // 2
    plane, core = section // 2, section % 2
    y, x = place // SIDE, place % SIDE
    group, member = (y // 2) * 2 + x // 2, (y % 2) * 2 + x % 2
    start = jnp.asarray(STARTS, jnp.int32)[group]

    def move(value, where):
        pairs = []
        for s in range(sections):
            for a in range(SIDE):
                for b in range(SIDE):
                    to, ta, tb = where(s, a, b)
                    pairs.append((
                        s * groups + a * SIDE + b,
                        (to % sections) * groups + (ta % SIDE) * SIDE + tb % SIDE,
                    ))
        return lax.ppermute(value, AXES, pairs)

    def swap_cores(value):
        return move(value, lambda s, a, b: (s ^ 1, a, b))

    def pack(h):
        width = w_query.shape[2] // 2
        cols = slice(h * width, (h + 1) * width)
        rows = w_output[0, cols]
        blocks = [rows[:, b * width : (b + 1) * width] for b in range(model // width)]
        return (
            jnp.concatenate([w_query[0, :, cols], w_key[0, :, cols]], axis=0),
            jnp.concatenate([w_value[0, :, cols]] + blocks, axis=0),
        )

    first = core == 0
    low, high = pack(0), pack(1)
    kept = [jnp.where(first, p, q) for p, q in zip(low, high)]
    got = [swap_cores(jnp.where(first, q, p)) for p, q in zip(low, high)]
    got_gain = swap_cores(norm_gain)
    gain_a, gain_b = jnp.where(first, norm_gain, got_gain), jnp.where(first, got_gain, norm_gain)

    def over_x(value):
        return move(value, lambda s, a, b: (s, a, b ^ 3))

    def over_y(value):
        return move(value, lambda s, a, b: (s, a ^ 3, b))

    def near(top, bottom):
        return [over_x(top), over_y(bottom), over_x(bottom), over_y(top)]

    def shards_of(own, x_top, y_bottom, x_bottom, y_top):
        far = [over_y(x_top), over_x(y_bottom)]
        return settle(own) + [x_top, x_bottom, y_top, y_bottom] + far

    own_a = [jnp.where(first, p, q) for p, q in zip(kept, got)]
    own_b = [jnp.where(first, q, p) for p, q in zip(kept, got)]
    near_a = near(*own_a)
    own_b, near_a[:2], segments = lax.optimization_barrier((own_b, near_a[:2], segment_ids))
    weights_a = shards_of(own_a, *near_a)
    weights_b = shards_of(own_b, *near(*own_b))

    inputs_all = lax.all_gather(inputs, "dp", axis=1, tiled=True)
    window_mine = lax.dynamic_slice_in_dim(inputs_all, start + HALF * core, HALF, 1)
    window_other = lax.dynamic_slice_in_dim(inputs_all, start + HALF * (1 - core), HALF, 1)

    slots = place * row_count + jnp.arange(row_count, dtype=jnp.int32)
    holders = [
        jnp.sum(
            (slots[:, None] >= group_bounds(segments[m])[None, 1:]).astype(jnp.int32), axis=1
        )
        for m in range(micro_count)
    ]
    window_mine, holders = lax.optimization_barrier((window_mine, holders))

    biases = jnp.stack([
        window_masks(segment_ids[m], prefix_lengths[m], batch_lengths[m], start, core)
        for m in range(micro_count)
    ])
    where_am_i = jnp.concatenate([
        jnp.stack([plane, core, start]).astype(jnp.int32), batch_lengths.astype(jnp.int32)
    ])

    def one_layer(turn, mine, other, gain, weights):
        keep, send = run_layer(turn, where_am_i, mine, other, gain, biases, weights)
        chip = (
            keep.astype(jnp.float32) + swap_cores(send).astype(jnp.float32)
        ).astype(jnp.bfloat16)
        total = mine.astype(jnp.float32) + chip.astype(jnp.float32)
        for piece in (
            move(chip, lambda s, a, b: (s, a ^ 1, b ^ 1)),
            move(chip, lambda s, a, b: (s, a ^ 1, b)),
            move(chip, lambda s, a, b: (s, a, b ^ 1)),
        ):
            total = total + piece.astype(jnp.float32)
        return total.astype(jnp.bfloat16)

    own_at = quarter * group + row_count * member - start
    side = jnp.where(member < SIDE // 2, group + 1, group - 1)
    side_at = (quarter * side + row_count * member - start) % WINDOW
    at = jnp.where(own_at // HALF == core, own_at, side_at) % HALF
    blank = jnp.zeros((row_count, model), jnp.bfloat16)
    stash = [[blank] * micro_count, [blank] * micro_count]

    def keep_block(layer, turn, rows):
        found = lax.dynamic_slice_in_dim(rows, at, row_count, 0)
        for m in range(micro_count):
            if 0 <= turn - m < planes:
                stash[layer][m] = jnp.where(plane == turn - m, found, stash[layer][m])

    mine, other = window_mine[0], window_other[0]
    turns = planes + micro_count - 1
    for turn in range(turns):
        out_a = one_layer(turn, mine, other, gain_a, weights_a)
        out_b = one_layer(turn, out_a, swap_cores(out_a), gain_b, weights_b)
        if turn < turns - 1:
            onward = (
                jnp.where(plane == planes - 1, window_mine[1], out_b) if turn == 0 else out_b
            )
            mine = move(onward, lambda s, a, b: (s + 2, a, b))
            other = swap_cores(mine)
        keep_block(0, turn, out_a)
        keep_block(1, turn, out_b)

    def owner(s, a, b):
        g, t = (a // 2) * 2 + b // 2, (a % 2) * 2 + b % 2
        lower = t < SIDE // 2
        own_half = (quarter * g + row_count * t - STARTS[g]) // HALF
        to_core, to = (0 if lower else 1), g
        if s % 2 != own_half:
            to_core, to = 1 - to_core, (g + (1 if lower else -1)) % SIDE
        return (s - s % 2 + to_core, to, t)

    moved = move(jnp.stack([jnp.stack(rows) for rows in stash]), owner)
    stash_a, stash_b = moved[0], moved[1]
    here = jnp.where(first, stash_a, stash_b)
    there = swap_cores(jnp.where(first, stash_b, stash_a))
    has_own = first == (x < SIDE // 2)
    mine, other = jnp.where(has_own, here, there), jnp.where(has_own, there, here)
    picked = [
        jnp.where((holders[m] == y)[:, None], mine[m], other[m]) for m in range(micro_count)
    ]
    return jnp.stack(picked)[None]


def solution(mesh):
    return jax.shard_map(
        shards,
        mesh=mesh,
        in_specs=(
            P(None, "dp", None),
            P("section", None),
            P("section", None, "dp"),
            P("section", None, "dp"),
            P("section", None, "dp"),
            P("section", "dp", None),
            P(),
            P(),
            P(),
        ),
        out_specs=P("section", None, "dp", None),
        check_vma=False,
    )
```
